512 devices in a mesh: dp: 32 (over z, x_hi, core), clus: 16 (over x_lo, y).
Axes of the slice: x: 4 (x_hi: 2, x_lo: 2; x = x_hi * 2 + x_lo), y: 8, z: 8, core: 2. Of those that a mesh axis runs over, the one named last changes fastest.
Arguments:
- rows: bfloat16 [131072, 1024], P(('dp', 'clus')), may hold values from -8 to 8
- fine_assign: int32 [131072], P(('dp', 'clus')), may hold values from 0 to 131071, as said below
- parent1: int32 [131072], P(('dp', 'clus')), may hold values from 0 to 8191, as said below
- parent2: int32 [8192], P('dp'), may hold values from 0 to 511
- parent3: int32 [512], replicated, may hold values from 0 to 63
- shrink: float32 [4], replicated, may hold values from 0.5 to 2
Outputs:
- fine_centroids: bfloat16 [131072, 1024], P(('dp', 'clus'))
- mid_centroids: bfloat16 [8192, 1024], P(('dp', 'clus'))
- coarse_centroids: bfloat16 [512, 1024], P(('dp', 'clus'))
- spread: float32 [131072], P(('dp', 'clus'))
The draws below stay inside these ranges and needn't reach their ends.
Inputs may be any that keep to these rules, and one draw needn't show every extreme that they name: `fine_assign`: devices are numbered d = dp index * 16 + clus index, and fine centroid k is owned by device k // 256. Every row of device d names a fine centroid owned by a device of the same dp index. At most 32 rows of one device name centroids of one owner, and in every dp group some owner is named by exactly 32 rows of each device of the group. parent1[k] is one of the 256 second-level centroids g * 256 to g * 256 + 255, with g = k // 4096.
All inputs are finite; a program needn't handle non-finite values.
Results may differ from the reference program's by a relative error of at most 0.0035.
Values may be sent and summed in bfloat16 or wider, within the bound.
No kernel may reach another device: no remote copies, remote signals or barrier semaphores. Data moves between devices by JAX's collectives and lax.ppermute only.
A program may use at most 64 MiB of HBM per device.

```python
import math
import jax
import jax.numpy as jnp

D = 1024
ROWS_DEV = 256
F1 = 256
F2 = 256
K3 = 512
K4 = 64
ROWS = 131072
K1 = 131072
K2 = 8192
N_DP = 32
N_CLUS = 16
DEVICES = 512


def make_parent1(key):
    index = jnp.arange(F1 * DEVICES, dtype=jnp.int32)
    group = index // (F1 * N_CLUS)
    pick = jax.random.randint(jax.random.fold_in(key, 11), (F1 * DEVICES,), 0, F2)
    return (group * F2 + pick).astype(jnp.int32)


def make_parent2(key):
    return jax.random.randint(jax.random.fold_in(key, 12), (F2 * N_DP,), 0, K3).astype(jnp.int32)


def make_parent3(key):
    return jax.random.randint(jax.random.fold_in(key, 13), (K3,), 0, K4).astype(jnp.int32)


def make_assign(key):
    base = jax.random.fold_in(key, 14)
    key_full, key_position, key_order, key_local = jax.random.split(base, 4)
    capacity_limit = 2 * ROWS_DEV // N_CLUS
    position_count = N_CLUS * capacity_limit
    full_row = jax.random.randint(key_full, (N_DP,), 0, N_CLUS)
    complete_per_shard = jnp.repeat(full_row, N_CLUS)
    position_index = jnp.arange(position_count, dtype=jnp.int32)
    random_jitter = jax.random.randint(key_position, (DEVICES, position_count), 0, 2 ** 14)
    extra_reward = jnp.where(position_index[None, :] // capacity_limit == complete_per_shard[:, None], 2 ** 28, 0)
    rating_value = random_jitter * position_count + position_index[None, :] + extra_reward
    chosen = jnp.argsort(-rating_value, axis=1)[:, :ROWS_DEV]
    target = (chosen // capacity_limit).astype(jnp.int32)
    mixing = jax.random.randint(key_order, (DEVICES, ROWS_DEV), 0, 2 ** 14) * ROWS_DEV + jnp.arange(ROWS_DEV)[None, :]
    order = jnp.argsort(mixing, axis=1)
    target = jnp.take_along_axis(target, order, axis=1)
    local = jax.random.randint(key_local, (DEVICES, ROWS_DEV), 0, F1)
    dev_dp = (jnp.arange(DEVICES, dtype=jnp.int32) // N_CLUS)[:, None]
    fine = (dev_dp * N_CLUS + target) * F1 + local
    return fine.reshape(-1).astype(jnp.int32)


def offsets(key, labels):
    return jax.vmap(lambda label: jax.random.normal(jax.random.fold_in(key, label), (D,), jnp.float32))(labels)


def draw_fine_assign(key, part):
    return make_assign(key)


def draw_parent1(key, part):
    return make_parent1(key)


def draw_parent2(key, part):
    return make_parent2(key)


def draw_parent3(key, part):
    return make_parent3(key)


def draw_rows(key, part):
    first = make_assign(key)
    second = make_parent1(key)[first]
    third = make_parent2(key)[second]
    fourth = make_parent3(key)[third]
    values = offsets(jax.random.fold_in(key, 21), fourth)
    values = values + 0.8 * offsets(jax.random.fold_in(key, 22), third)
    values = values + 0.6 * offsets(jax.random.fold_in(key, 23), second)
    values = values + 0.5 * offsets(jax.random.fold_in(key, 24), first)
    values = values + 0.5 * jax.random.normal(jax.random.fold_in(key, 25), (ROWS_DEV * DEVICES, D), jnp.float32)
    return jnp.clip(values, -8.0, 8.0).astype(jnp.bfloat16)


def setup_inputs(seed: int = 0) -> dict:
    key_of = jax.random.split(jax.random.key(seed), 7)
    rows = draw_rows(jax.random.fold_in(key_of[6], 71), 0)
    fine_assign = draw_fine_assign(jax.random.fold_in(key_of[6], 71), 0)
    parent1 = draw_parent1(jax.random.fold_in(key_of[6], 71), 0)
    parent2 = draw_parent2(jax.random.fold_in(key_of[6], 71), 0)
    parent3 = draw_parent3(jax.random.fold_in(key_of[6], 71), 0)
    shrink = jnp.clip(jnp.exp(jax.random.uniform(key_of[5], (4,), jnp.float32, math.log(0.5), math.log(2.0))), 0.5, 2.0)
    return dict(rows=rows, fine_assign=fine_assign, parent1=parent1, parent2=parent2, parent3=parent3, shrink=shrink)


def shrunk(sums, counts, prior, weight):
    return (sums + weight * prior) / (counts + weight)[:, None]


def reference(rows, fine_assign, parent1, parent2, parent3, shrink):
    ones = jnp.ones(fine_assign.shape, jnp.float32)
    fine_sums = jax.ops.segment_sum(rows.astype(jnp.float32), fine_assign, num_segments=K1)
    fine_counts = jax.ops.segment_sum(ones, fine_assign, num_segments=K1)
    middle_sums = jax.ops.segment_sum(fine_sums, parent1, num_segments=K2)
    middle_counts = jax.ops.segment_sum(fine_counts, parent1, num_segments=K2)
    third_sums = jax.ops.segment_sum(middle_sums, parent2, num_segments=K3)
    third_counts = jax.ops.segment_sum(middle_counts, parent2, num_segments=K3)
    top_sums = jax.ops.segment_sum(third_sums, parent3, num_segments=K4)
    top_counts = jax.ops.segment_sum(third_counts, parent3, num_segments=K4)
    center = jnp.sum(top_sums, axis=0) / ROWS
    top_means = shrunk(top_sums, top_counts, center[None, :], shrink[0] * (ROWS / K4))
    third_means = shrunk(third_sums, third_counts, top_means[parent3], shrink[1] * (ROWS / K3))
    middle_means = shrunk(middle_sums, middle_counts, third_means[parent2], shrink[2] * (ROWS / K2))
    fine_means = shrunk(fine_sums, fine_counts, middle_means[parent1], shrink[3] * (ROWS / K1))
    fine_out = fine_means.astype(jnp.bfloat16)
    diff = rows.astype(jnp.float32) - fine_out.astype(jnp.float32)[fine_assign]
    error = jnp.sum(diff * diff, axis=1)
    spread = jax.ops.segment_sum(error, fine_assign, num_segments=K1) / (D * (fine_counts + 1.0))
    return fine_out, middle_means.astype(jnp.bfloat16), third_means.astype(jnp.bfloat16), spread
```

```python
import jax
import jax.numpy as jnp
from jax import lax
from jax.experimental import pallas as pl
from jax.experimental.pallas import tpu as pltpu
from jax.sharding import PartitionSpec as P

GROUPS = 16
DP = 32
FINE = 256
MIDDLE = 256
THIRD = 512
TOP = 64
WIDTH = 1024
PART = WIDTH // GROUPS
TOTAL = 131072.0
BF = jnp.bfloat16
F32 = jnp.float32
I32 = jnp.int32
LIMIT = 24 * 1024 * 1024


def iota(shape, dim):
    return lax.broadcasted_iota(I32, shape, dim)


def hot(mask):
    return jnp.where(mask, 1.0, 0.0).astype(BF)


def pieces(x, count):
    out = []
    for k in range(count):
        part = x.astype(BF)
        out.append(part)
        if k + 1 < count:
            x = x - part.astype(F32)
    return out


def turned(x):
    return pltpu.roll(x, PART, 1)


def dot(a, b):
    return jnp.dot(a, b, preferred_element_type=F32)


def dot_first(a, b):
    return lax.dot_general(a, b, (((0,), (0,)), ((), ())), preferred_element_type=F32)


def summed(x, count):
    total = x[:, 0:128]
    for k in range(1, count):
        total = total + x[:, 128 * k : 128 * (k + 1)]
    return total


def in_line(ref, first, count):
    return jnp.concatenate([ref[first + k : first + k + 1, :] for k in range(count)], axis=1)


def pack_kernel(rows_ref, assign_ref, parent1_ref, send_ref, ids_ref):
    left = iota((128, 128), 1) < PART
    for g in range(GROUPS // 2):
        top = rows_ref[0:128, 128 * g : 128 * (g + 1)].astype(F32)
        low = rows_ref[128:256, 128 * g : 128 * (g + 1)].astype(F32)
        send_ref[2 * g] = jnp.where(left, top, turned(low)).astype(BF)
        send_ref[2 * g + 1] = jnp.where(left, turned(top), low).astype(BF)
    fine = (assign_ref[...] & (GROUPS * FINE - 1)).astype(F32)
    parent = (parent1_ref[...] & (MIDDLE - 1)).astype(F32)
    tile = jnp.concatenate([fine, parent, jnp.zeros((4, 128), F32)], axis=0)
    ids_ref[...] = jnp.broadcast_to(tile[None], (GROUPS, 8, 128))


def middle_kernel(rows_ref, ids_ref, parent2_ref, third_ref, middle_ref, tally_ref, hot_ref):
    left = iota((256, 128), 1) < PART
    table = jnp.concatenate([ids_ref[:, 2, :], ids_ref[:, 3, :]], axis=1).astype(BF)
    down = iota((256, 128), 0)
    owner = iota((GROUPS, 128), 0)
    for s in range(GROUPS):
        for j in range(2):
            fine = ids_ref[s, j : j + 1, :].astype(I32)
            found = dot(table, hot(down == (fine & (FINE - 1))))
            parent = jnp.sum(jnp.where(owner == (fine >> 8), found, 0.0), axis=0, keepdims=True)
            hot_ref[256 * j : 256 * (j + 1), 128 * s : 128 * (s + 1)] = hot(
                down == parent.astype(I32)
            )
    both = dot(hot_ref[...], rows_ref[...].reshape(GROUPS * 128, 128))
    middle = jnp.where(left, both[0:256], both[256:512])
    middle = middle + turned(middle)
    ones = jnp.ones((GROUPS * 128, 128), BF)
    tally = dot(hot_ref[0:256] + hot_ref[256:512], ones)
    middle_ref[...] = middle
    tally_ref[...] = tally
    line = in_line(parent2_ref, 0, 2)
    third = iota((256, 256), 0)
    parts = jnp.concatenate(pieces(middle, 3) + pieces(tally, 2), axis=1)
    first = dot(hot(third == line), parts)
    second = dot(hot(third + 256 == line), parts)
    sums = jnp.where(left, summed(first, 3), summed(second, 3))
    counts = jnp.where(left, summed(first[:, 384:], 2), summed(second[:, 384:], 2))
    third_ref[:, 0:8, :] = sums.reshape(DP, 8, 128)
    third_ref[:, 8:16, :] = counts.reshape(DP, 8, 128)


def fine_kernel(shrink_ref, rows_ref, ids_ref, sums_ref, inv_ref, count_ref, lines_ref, hot_ref, wide_ref, acc_ref):
    lane = iota((128, 128), 1)
    left = lane < PART
    half = jnp.where(left, 0, 1)
    group = lane >> 5
    down = iota((128, 128), 0)
    weight = shrink_ref[3]
    columns = jnp.transpose(ids_ref[...].reshape(128, 128)).astype(I32)
    for s in range(GROUPS):
        x = rows_ref[s].astype(F32)
        y = turned(x)
        ones = []
        for j in range(2):
            block = slice(128 * j, 128 * (j + 1))
            twice = jnp.where(left, x, y) if j == 0 else jnp.where(left, y, x)
            key = columns[:, 8 * s + j : 8 * s + j + 1] >> 7
            place = jnp.broadcast_to(key, (128, 128)) - half
            for h in range(GROUPS):
                wide_ref[block, 128 * h : 128 * (h + 1)] = jnp.where(
                    place == 2 * h, twice, 0.0
                ).astype(BF)
            square = 0.5 * jnp.sum(twice * twice, axis=1, keepdims=True)
            hi, mid, lo = [p.astype(F32) for p in pieces(jnp.broadcast_to(square, (128, 128)), 3)]
            value = jnp.where(group == 0, hi, jnp.where(group == 1, mid, jnp.where(group == 2, lo, 1.0)))
            wide_ref[block, 2048:2176] = jnp.where((lane & 31) == key, value, 0.0).astype(BF)
            fine = ids_ref[s, j : j + 1, :].astype(I32)
            ones.append(hot(down == (fine & 127)))
        part = dot(jnp.concatenate(ones, axis=1), wide_ref[...])
        acc_ref[...] = part if s == 0 else acc_ref[...] + part
    sums_ref[...] = acc_ref[:, 0:2048]
    tail = acc_ref[:, 2048:2176]
    square = tail[:, 0:32] + tail[:, 32:64] + tail[:, 64:96]
    count = tail[:, 96:128]
    lines_ref[...] = jnp.transpose(
        jnp.concatenate([square, count, jnp.zeros((128, 64), F32)], axis=1)
    )
    inverse = 1.0 / (count + weight)
    across = iota((128, 256), 1)
    for h in range(GROUPS):
        here = slice(128 * h, 128 * (h + 1))
        inv_ref[:, here] = jnp.where(left, inverse[:, 2 * h : 2 * h + 1], inverse[:, 2 * h + 1 : 2 * h + 2])
        count_ref[:, here] = jnp.where(left, count[:, 2 * h : 2 * h + 1], count[:, 2 * h + 1 : 2 * h + 2])
        for b in range(2):
            parent = columns[:, 8 * h + 2 + b : 8 * h + 3 + b]
            hot_ref[256 * h + 128 * b : 256 * h + 128 * (b + 1), :] = hot(across == parent)


def spread_out_kernel(got_ref, out_ref):
    total = got_ref[0]
    for k in range(1, DP):
        total = total + got_ref[k]
    out_ref[...] = jnp.broadcast_to(total[None], (DP, 16, 128))


def down_kernel(
    shrink_ref, dp_ref, got_ref, parent2_ref, parent3_ref, middle_ref, tally_ref, sums_ref, inv_ref,
    count_ref, lines_ref, hot_ref, fine_ref, small_ref, third_ref, diff_ref,
):
    left = iota((256, 128), 1) < PART
    weight_top = shrink_ref[0] * (TOTAL / TOP)
    weight_third = shrink_ref[1] * (TOTAL / THIRD)
    weight_middle = shrink_ref[2] * (TOTAL / 8192)
    weight_fine = shrink_ref[3]
    third_sums = got_ref[:, 0:8, :].reshape(256, 128)
    third_counts = got_ref[:, 8:16, :].reshape(256, 128)
    top_id = iota((TOP, 256), 0)
    hot_first = hot(top_id == in_line(parent3_ref, 0, 2))
    hot_second = hot(top_id == in_line(parent3_ref, 2, 2))
    parts = jnp.concatenate(pieces(third_sums, 3) + pieces(third_counts, 3), axis=1)
    first = dot(hot_first, parts)
    second = dot(hot_second, parts)
    top = jnp.where(left[0:TOP], summed(first, 3), summed(second, 3))
    top = top + turned(top)
    top_counts = jnp.where(left[0:TOP], summed(first[:, 384:], 3), summed(second[:, 384:], 3))
    top_counts = top_counts + turned(top_counts)
    center = jnp.sum(top, axis=0, keepdims=True) / TOTAL
    top_means = (top + weight_top * center) / (top_counts + weight_top)
    parts = jnp.concatenate(pieces(top_means, 3), axis=1)
    prior = jnp.where(
        left, summed(dot_first(hot_first, parts), 3), summed(dot_first(hot_second, parts), 3)
    )
    third_means = (third_sums + weight_third * prior) / (third_counts + weight_third)
    third_ref[...] = third_means
    line = in_line(parent2_ref, 0, 2)
    third_id = iota((256, 256), 0)
    parts = jnp.concatenate(pieces(third_means, 3), axis=1)
    prior = jnp.where(
        left,
        summed(dot_first(hot(third_id == line), parts), 3),
        summed(dot_first(hot(third_id + 256 == line), parts), 3),
    )
    prior = prior + turned(prior)
    middle_means = (middle_ref[...] + weight_middle * prior) / (tally_ref[...] + weight_middle)
    parts = jnp.concatenate(pieces(middle_means, 2), axis=1)
    left = left[0:128]
    for h in range(GROUPS):
        here = slice(128 * h, 128 * (h + 1))
        found = summed(dot(hot_ref[256 * h : 256 * (h + 1), :], parts), 2)
        prior = jnp.where(left, found[0:128], found[128:256])
        sums = sums_ref[:, here]
        fine = ((sums + weight_fine * prior) * inv_ref[:, here]).astype(BF)
        fine_ref[h] = fine
        fine = fine.astype(F32)
        hi, lo = pieces(fine * (count_ref[:, here] * fine - 2.0 * sums), 2)
        diff_ref[:, here] = hi
        diff_ref[:, 2048 + 128 * h : 2048 + 128 * (h + 1)] = lo
    select = hot((iota((2048, 128), 0) >> 6) == iota((2048, 128), 1))
    diff = dot(diff_ref[:, 0:2048], select) + dot(diff_ref[:, 2048:4096], select)
    spread = jnp.transpose(diff)[0:32] + lines_ref[0:32]
    counts = lines_ref[32:64]
    dp = dp_ref[0]
    own = third_ref[pl.ds(pl.multiple_of((dp % 16) * 16, 16), 16), :]
    own = jnp.where(dp < 16, own, turned(own))
    for h in range(GROUPS):
        small_ref[h, 0:8, :] = jnp.where(
            left[0:8], middle_means[16 * h : 16 * h + 8], middle_means[16 * h + 8 : 16 * h + 16]
        )
        small_ref[h, 8:16, :] = jnp.concatenate(
            [
                own[h : h + 1],
                spread[2 * h : 2 * h + 2],
                counts[2 * h : 2 * h + 2],
                jnp.zeros((3, 128), F32),
            ],
            axis=0,
        )


def finish_kernel(fine_ref, small_ref, out_ref, middle_ref, third_ref, spread_ref):
    left = iota((128, 128), 1) < PART
    for g in range(GROUPS // 2):
        here = slice(128 * g, 128 * (g + 1))
        a = fine_ref[2 * g].astype(F32)
        b = fine_ref[2 * g + 1].astype(F32)
        out_ref[0:128, here] = jnp.where(left, a, turned(b)).astype(BF)
        out_ref[128:256, here] = jnp.where(left, turned(a), b).astype(BF)
        a = small_ref[2 * g]
        b = small_ref[2 * g + 1]
        first = jnp.where(left[0:16], a, turned(b))
        second = jnp.where(left[0:16], turned(a), b)
        middle_ref[:, here] = jnp.concatenate([first[0:8], second[0:8]], axis=0).astype(BF)
        third_ref[:, here] = first[8:9].astype(BF)
    total = small_ref[0, 8:16, :]
    counts = total[3:5]
    for k in range(1, GROUPS):
        total = total + small_ref[k, 8:16, :]
    spread_ref[...] = total[1:3] / (WIDTH * (counts + 1.0))


VMEM = pl.BlockSpec(memory_space=pltpu.VMEM)
SMEM = pl.BlockSpec(memory_space=pltpu.SMEM)


def call(kernel, ins, outs, scratch=(), cost=(0, 0)):
    return pl.pallas_call(
        kernel,
        out_shape=[jax.ShapeDtypeStruct(s, d) for s, d in outs],
        in_specs=ins,
        out_specs=[VMEM] * len(outs),
        scratch_shapes=[pltpu.VMEM(s, d) for s, d in scratch],
        compiler_params=pltpu.CompilerParams(vmem_limit_bytes=LIMIT),
        cost_estimate=pl.CostEstimate(flops=cost[0], bytes_accessed=cost[1], transcendentals=0),
    )


def exchange(x, axis):
    return lax.all_to_all(x, axis, split_axis=0, concat_axis=0, tiled=True)


def local(rows, fine_assign, parent1, parent2, parent3, shrink):
    dp = lax.axis_index("dp").astype(I32).reshape(1)
    parent2 = parent2.reshape(2, 128)
    parent3 = parent3.reshape(4, 128)
    send, ids = call(
        pack_kernel, [VMEM] * 3, [((GROUPS, 128, 128), BF), ((GROUPS, 8, 128), F32)]
    )(rows, fine_assign.reshape(2, 128), parent1.reshape(2, 128))
    ids = exchange(ids, "clus")
    group_rows = exchange(send, "clus")
    third, middle, tally = call(
        middle_kernel,
        [VMEM] * 3,
        [((DP, 16, 128), F32), ((256, 128), F32), ((256, 128), F32)],
        [((512, 2048), BF)],
    )(group_rows, ids, parent2)
    third = exchange(third, "dp")
    sums, inverse, counts, lines, parents = call(
        fine_kernel,
        [SMEM, VMEM, VMEM],
        [((128, 2048), F32), ((128, 2048), F32), ((128, 2048), F32), ((128, 128), F32), ((4096, 256), BF)],
        [((256, 2176), BF), ((128, 2176), F32)],
        (4_000_000_000, 4_000_000),
    )(shrink, group_rows, ids)
    (third,) = call(spread_out_kernel, [VMEM], [((DP, 16, 128), F32)])(third)
    third = exchange(third, "dp")
    fine, small = call(
        down_kernel,
        [SMEM, SMEM] + [VMEM] * 10,
        [((GROUPS, 128, 128), BF), ((GROUPS, 16, 128), F32)],
        [((256, 128), F32), ((128, 4096), BF)],
    )(shrink, dp, third, parent2, parent3, middle, tally, sums, inverse, counts, lines, parents)
    fine = exchange(fine, "clus")
    small = exchange(small, "clus")
    fine, middle, third, spread = call(
        finish_kernel,
        [VMEM] * 2,
        [((256, 1024), BF), ((16, 1024), BF), ((1, 1024), BF), ((2, 128), F32)],
    )(fine, small)
    return fine, middle, third, spread.reshape(256)


def solution(mesh):
    placed = (P(("dp", "clus"), None), P(("dp", "clus")), P(("dp", "clus")), P("dp"), P(), P())
    return jax.shard_map(
        local,
        mesh=mesh,
        in_specs=placed,
        out_specs=(
            P(("dp", "clus"), None),
            P(("dp", "clus"), None),
            P(("dp", "clus"), None),
            P(("dp", "clus")),
        ),
        check_vma=False,
    )
```

```python
import jax
import jax.numpy as jnp
from jax import lax
from jax.experimental import pallas as pl
from jax.experimental.pallas import tpu as pltpu
from jax.sharding import PartitionSpec as P

GROUPS = 16
DP = 32
FINE = 256
MIDDLE = 256
THIRD = 512
TOP = 64
WIDTH = 1024
PART = WIDTH // GROUPS
ROWS = 144
TOTAL = 131072.0
BF = jnp.bfloat16
F32 = jnp.float32
I32 = jnp.int32
MIB = 1024 * 1024


def iota(shape, dim):
    return lax.broadcasted_iota(I32, shape, dim)


def hot(mask):
    return jnp.where(mask, 1.0, 0.0).astype(BF)


def pieces(x, count):
    out = []
    for k in range(count):
        part = x.astype(BF)
        out.append(part)
        if k + 1 < count:
            x = x - part.astype(F32)
    return out


def side(x, count):
    return jnp.concatenate(pieces(x, count), axis=1)


def turned(x):
    return pltpu.roll(x, PART, 1)


def dot(a, b):
    return jnp.dot(a, b, preferred_element_type=F32)


def dot_last(a, b):
    return lax.dot_general(a, b, (((1,), (1,)), ((), ())), preferred_element_type=F32)


def two(x):
    return x[:, 0:128] + x[:, 128:256]


def in_line(ref, first, count):
    return jnp.concatenate([ref[first + k : first + k + 1, :] for k in range(count)], axis=1)


def pack_kernel(rows_hbm, assign_hbm, parent1_hbm, send_ref, rows_ref, assign_ref, parent1_ref, sems):
    copies = [
        pltpu.make_async_copy(src, dst, sems.at[k])
        for k, (src, dst) in enumerate(
            [(rows_hbm, rows_ref), (assign_hbm, assign_ref), (parent1_hbm, parent1_ref)]
        )
    ]
    for copy in copies:
        copy.start()
    copies[1].wait()
    copies[2].wait()
    fine = assign_ref[...] & (GROUPS * FINE - 1)
    parent = parent1_ref[...] & (MIDDLE - 1)
    tile = jnp.concatenate(
        [
            (fine >> 8).astype(F32),
            (fine & (FINE - 1)).astype(F32),
            parent.astype(F32),
            jnp.zeros((10, 128), F32),
        ],
        axis=0,
    ).astype(BF)
    for k in range(GROUPS):
        send_ref[k, 128:144, :] = tile
    copies[0].wait()
    left = iota((128, 128), 1) < PART
    for g in range(GROUPS // 2):
        top = rows_ref[0:128, 128 * g : 128 * (g + 1)].astype(F32)
        low = rows_ref[128:256, 128 * g : 128 * (g + 1)].astype(F32)
        send_ref[2 * g, 0:128, :] = jnp.where(left, top, turned(low)).astype(BF)
        send_ref[2 * g + 1, 0:128, :] = jnp.where(left, turned(top), low).astype(BF)


def middle_kernel(rows_ref, parent2_hbm, third_ref, middle_ref, line_ref, ids_ref, hot_ref, parent2_ref, sem):
    copy = pltpu.make_async_copy(parent2_hbm, parent2_ref, sem)
    copy.start()
    left = iota((256, 128), 1) < PART
    tails = [rows_ref[s, 128:144, :].astype(F32)[0:8] for s in range(GROUPS)]
    for s in range(GROUPS):
        ids_ref[8 * s : 8 * s + 8, :] = tails[s]
    table = jnp.concatenate(
        [jnp.concatenate([tail[k : k + 1] for tail in tails], axis=0) for k in (4, 5)], axis=1
    ).astype(BF)
    down = iota((256, 128), 0)
    owner = iota((GROUPS, 128), 0)
    for s in range(GROUPS):
        tail = tails[s].astype(I32)
        for j in range(2):
            found = dot(table, hot(down == tail[2 + j : 3 + j]))
            parent = jnp.sum(jnp.where(owner == tail[j : j + 1], found, 0.0), axis=0, keepdims=True)
            hot_ref[256 * j : 256 * (j + 1), 128 * s : 128 * (s + 1)] = hot(
                down == parent.astype(I32)
            )
    both = dot(hot_ref[...], rows_ref[:, 0:128, :].reshape(GROUPS * 128, 128))
    middle = jnp.where(left, both[0:256], both[256:512])
    middle = middle + turned(middle)
    tally = dot_last(jnp.ones((8, 2048), BF), hot_ref[0:256] + hot_ref[256:512])
    middle_ref[...] = middle
    line_ref[...] = tally
    copy.wait()
    line = in_line(parent2_ref, 0, 2)
    third = iota((256, 256), 0)
    first = hot(third == line)
    second = hot(third + 256 == line)
    parts = side(middle, 2)
    sums = jnp.where(left, two(dot(first, parts)), two(dot(second, parts))).reshape(DP, 8, 128)
    third_ref[:, 0] = sums[:, 0:4]
    third_ref[:, 1] = sums[:, 4:8]
    high, low = pieces(tally, 2)
    for k, ones in enumerate((first, second)):
        count = dot_last(high, ones) + dot_last(low, ones)
        for i in range(2):
            third_ref[:, 2, 2 * k + i, :] = jnp.broadcast_to(
                count[0:1, 128 * i : 128 * (i + 1)], (DP, 128)
            )


def fine_kernel(rows_ref, ids_ref, acc_ref, wide_ref):
    lane = iota((128, 128), 1)
    left = lane < PART
    half = jnp.where(left, 0.0, 1.0)
    group = lane >> 5
    down = iota((128, 128), 0)
    columns = jnp.transpose(ids_ref[...])
    for s in range(GROUPS):
        x = rows_ref[s, 0:128, :].astype(F32)
        y = turned(x)
        ones = []
        for j in range(2):
            block = slice(128 * j, 128 * (j + 1))
            twice = jnp.where(left, x, y) if j == 0 else jnp.where(left, y, x)
            low = columns[:, 8 * s + 2 + j : 8 * s + 3 + j]
            key = 2.0 * columns[:, 8 * s + j : 8 * s + j + 1] + jnp.where(low >= 128.0, 1.0, 0.0)
            key = jnp.broadcast_to(key, (128, 128))
            place = (key - half).astype(BF)
            narrow = twice.astype(BF)
            for h in range(GROUPS):
                wide_ref[block, 128 * h : 128 * (h + 1)] = jnp.where(
                    place == jnp.array(2 * h, BF), narrow, jnp.array(0, BF)
                )
            square = 0.5 * jnp.sum(twice * twice, axis=1, keepdims=True)
            hi, mid, lo = [p.astype(F32) for p in pieces(jnp.broadcast_to(square, (128, 128)), 3)]
            value = jnp.where(group == 0, hi, jnp.where(group == 1, mid, jnp.where(group == 2, lo, 1.0)))
            wide_ref[block, 2048:2176] = jnp.where(
                (lane & 31) == key.astype(I32), value, 0.0
            ).astype(BF)
            within = ids_ref[8 * s + 2 + j : 8 * s + 3 + j, :].astype(I32) & 127
            ones.append(hot(down == within))
        part = dot(jnp.concatenate(ones, axis=1), wide_ref[...])
        acc_ref[...] = part if s == 0 else acc_ref[...] + part


def share_kernel(got_ref, acc_hbm, out_ref, count_ref):
    total = got_ref[0]
    for k in range(1, DP):
        total = total + got_ref[k]
    sums = jnp.concatenate([total[0], total[1]], axis=0)
    out_ref[...] = jnp.broadcast_to(sums[None], (DP, 8, 128))
    count_ref[...] = total[2]


def ready_kernel(
    shrink_ref, acc_ref, ids_ref, line_ref, third_ref, parent2_ref, parent3_ref, inv_ref, count_ref,
    lines_ref, hot_ref, third_inv_ref, top_inv_ref, middle_inv_ref, top_hot_ref, top_turn_ref, middle_turn_ref,
):
    weight_top = shrink_ref[0] * (TOTAL / TOP)
    weight_third = shrink_ref[1] * (TOTAL / THIRD)
    weight_middle = shrink_ref[2] * (TOTAL / 8192)
    weight_fine = shrink_ref[3]
    left = iota((256, 128), 1) < PART
    columns = jnp.transpose(ids_ref[...])
    tail = acc_ref[:, 2048:2176]
    square = tail[:, 0:32] + tail[:, 32:64] + tail[:, 64:96]
    count = tail[:, 96:128]
    lines_ref[...] = jnp.transpose(
        jnp.concatenate([square, count, jnp.zeros((128, 64), F32)], axis=1)
    )
    inverse = 1.0 / (count + weight_fine)
    across = iota((128, 256), 1)
    for h in range(GROUPS):
        here = slice(128 * h, 128 * (h + 1))
        pair = (slice(2 * h, 2 * h + 1), slice(2 * h + 1, 2 * h + 2))
        inv_ref[:, here] = jnp.where(left[0:128], inverse[:, pair[0]], inverse[:, pair[1]])
        count_ref[:, here] = jnp.where(left[0:128], count[:, pair[0]], count[:, pair[1]])
        for b in range(2):
            parent = columns[:, 8 * h + 4 + b : 8 * h + 5 + b].astype(I32)
            hot_ref[256 * h + 128 * b : 256 * h + 128 * (b + 1), :] = hot(across == parent)
    tally = line_ref[0:1, :]
    lines = jnp.concatenate(
        [
            third_ref[...],
            tally[:, 0:128],
            tally[:, 128:256],
            parent2_ref[...].astype(F32),
            parent3_ref[...].astype(F32),
            jnp.zeros((116, 128), F32),
        ],
        axis=0,
    )
    columns = jnp.transpose(lines)
    first = jnp.concatenate([columns[:, 0:1], columns[:, 1:2]], axis=0)
    second = jnp.concatenate([columns[:, 2:3], columns[:, 3:4]], axis=0)
    counts = jnp.where(left, first, second)
    third_inv_ref[...] = 1.0 / (counts + weight_third)
    tally = jnp.concatenate([columns[:, 4:5], columns[:, 5:6]], axis=0)
    middle_inv_ref[...] = jnp.broadcast_to(1.0 / (tally + weight_middle), (256, 128))
    top_id = iota((TOP, 256), 0)
    top_first = hot(top_id == in_line(parent3_ref, 0, 2))
    top_second = hot(top_id == in_line(parent3_ref, 2, 2))
    top_hot_ref[0:TOP, :] = top_first
    top_hot_ref[TOP : 2 * TOP, :] = top_second
    parts = jnp.concatenate(pieces(counts, 3), axis=1)
    first = dot(top_first, parts)
    second = dot(top_second, parts)
    first = first[:, 0:128] + first[:, 128:256] + first[:, 256:384]
    second = second[:, 0:128] + second[:, 128:256] + second[:, 256:384]
    top = jnp.where(left[0:TOP], first, second)
    top_inv_ref[...] = 1.0 / (top + turned(top) + weight_top)
    parents = [columns[:, 6 + k : 7 + k].astype(I32) for k in range(6)]
    for k in range(2):
        for b in range(2):
            middle_turn_ref[256 * b + 128 * k : 256 * b + 128 * (k + 1), :] = hot(
                across + 256 * b == parents[k]
            )
    for k in range(4):
        top_turn_ref[128 * k : 128 * (k + 1), :] = hot(across[:, 0:128] == parents[2 + k])[:, 0:TOP]


def down_kernel(
    shrink_ref, dp_ref, got_ref, middle_ref, acc_ref, inv_ref, count_ref, lines_ref, hot_ref, third_inv_ref,
    top_inv_ref, middle_inv_ref, top_hot_ref, top_turn_ref, middle_turn_ref, send_ref, third_ref, diff_ref,
):
    left = iota((256, 128), 1) < PART
    weight_top = shrink_ref[0] * (TOTAL / TOP)
    weight_third = shrink_ref[1] * (TOTAL / THIRD)
    weight_middle = shrink_ref[2] * (TOTAL / 8192)
    weight_fine = shrink_ref[3]
    third_sums = got_ref[...].reshape(256, 128)
    top = two(dot(top_hot_ref[...], side(third_sums, 2)))
    top = jnp.where(left[0:TOP], top[0:TOP], top[TOP : 2 * TOP])
    top = top + turned(top)
    center = jnp.sum(top, axis=0, keepdims=True) / TOTAL
    top_means = (top + weight_top * center) * top_inv_ref[...]
    prior = two(dot(top_turn_ref[...], side(top_means, 2)))
    prior = jnp.where(left, prior[0:256], prior[256:512])
    third_means = (third_sums + weight_third * prior) * third_inv_ref[...]
    third_ref[...] = third_means
    prior = two(dot(middle_turn_ref[...], side(third_means, 2)))
    prior = jnp.where(left, prior[0:256], prior[256:512])
    prior = prior + turned(prior)
    middle_means = (middle_ref[...] + weight_middle * prior) * middle_inv_ref[...]
    parts = side(middle_means, 2)
    left = left[0:128]
    for h in range(GROUPS):
        here = slice(128 * h, 128 * (h + 1))
        found = two(dot(hot_ref[256 * h : 256 * (h + 1), :], parts))
        prior = jnp.where(left, found[0:128], found[128:256])
        sums = acc_ref[:, here]
        fine = ((sums + weight_fine * prior) * inv_ref[:, here]).astype(BF)
        send_ref[h, 0:128, :] = fine
        fine = fine.astype(F32)
        hi, lo = pieces(fine * (count_ref[:, here] * fine - 2.0 * sums), 2)
        diff_ref[:, here] = hi
        diff_ref[:, 2048 + 128 * h : 2048 + 128 * (h + 1)] = lo
    select = hot((iota((2048, 128), 0) >> 6) == iota((2048, 128), 1))
    diff = dot(diff_ref[:, 0:2048], select) + dot(diff_ref[:, 2048:4096], select)
    spread = jnp.transpose(diff)[0:32] + lines_ref[0:32]
    spread = [p.astype(F32) for p in pieces(spread, 3)]
    dp = dp_ref[0]
    own = third_ref[pl.ds(pl.multiple_of((dp % 16) * 16, 16), 16), :]
    own = jnp.where(dp < 16, own, turned(own))
    for h in range(GROUPS):
        send_ref[h, 128:144, :] = jnp.concatenate(
            [
                jnp.where(
                    left[0:8], middle_means[16 * h : 16 * h + 8], middle_means[16 * h + 8 : 16 * h + 16]
                ),
                own[h : h + 1],
                spread[0][2 * h : 2 * h + 2],
                spread[1][2 * h : 2 * h + 2],
                spread[2][2 * h : 2 * h + 2],
                jnp.zeros((1, 128), F32),
            ],
            axis=0,
        ).astype(BF)


def finish_kernel(clus_ref, got_ref, lines_ref, out_ref, middle_ref, third_ref, spread_ref):
    left = iota((128, 128), 1) < PART
    total = jnp.zeros((8, 128), F32)
    for g in range(GROUPS // 2):
        here = slice(128 * g, 128 * (g + 1))
        a = got_ref[2 * g, 0:128, :].astype(F32)
        b = got_ref[2 * g + 1, 0:128, :].astype(F32)
        out_ref[0:128, here] = jnp.where(left, a, turned(b)).astype(BF)
        out_ref[128:256, here] = jnp.where(left, turned(a), b).astype(BF)
        a = got_ref[2 * g, 128:144, :].astype(F32)
        b = got_ref[2 * g + 1, 128:144, :].astype(F32)
        first = jnp.where(left[0:16], a, turned(b))
        second = jnp.where(left[0:16], turned(a), b)
        middle_ref[:, here] = jnp.concatenate([first[0:8], second[0:8]], axis=0).astype(BF)
        third_ref[:, here] = first[8:9].astype(BF)
        total = total + a[8:16] + b[8:16]
    total = total[1:3] + total[3:5] + total[5:7]
    row = iota((32, 128), 0)
    counts = [
        jnp.sum(jnp.where(row == 2 * clus_ref[0] + b, lines_ref[32:64], 0.0), axis=0, keepdims=True)
        for b in range(2)
    ]
    spread_ref[...] = total / (WIDTH * (jnp.concatenate(counts, axis=0) + 1.0))


VMEM = pl.BlockSpec(memory_space=pltpu.VMEM)
SMEM = pl.BlockSpec(memory_space=pltpu.SMEM)
ANY = pl.BlockSpec(memory_space=pl.ANY)
DMA = pltpu.SemaphoreType.DMA


def call(kernel, limit, ins, outs, scratch=(), flops=0, moved=0):
    return pl.pallas_call(
        kernel,
        out_shape=[jax.ShapeDtypeStruct(s, d) for s, d in outs],
        in_specs=ins,
        out_specs=[VMEM] * len(outs),
        scratch_shapes=list(scratch),
        compiler_params=pltpu.CompilerParams(vmem_limit_bytes=limit * MIB),
        cost_estimate=pl.CostEstimate(flops=flops, bytes_accessed=moved, transcendentals=0),
    )


def exchange(x, axis):
    return lax.all_to_all(x, axis, split_axis=0, concat_axis=0, tiled=True)


def local(rows, fine_assign, parent1, parent2, parent3, shrink):
    dp = lax.axis_index("dp").astype(I32).reshape(1)
    clus = lax.axis_index("clus").astype(I32).reshape(1)
    parent2 = parent2.reshape(2, 128)
    parent3 = parent3.reshape(4, 128)
    block = ((GROUPS, ROWS, 128), BF)
    (send,) = call(
        pack_kernel,
        60,
        [ANY] * 3,
        [block],
        [
            pltpu.VMEM((256, WIDTH), BF),
            pltpu.VMEM((2, 128), I32),
            pltpu.VMEM((2, 128), I32),
            DMA((3,)),
        ],
    )(rows, fine_assign.reshape(2, 128), parent1.reshape(2, 128))
    group_rows = exchange(send, "clus")
    third, middle, line, ids = call(
        middle_kernel,
        32,
        [VMEM, ANY],
        [((DP, 3, 4, 128), F32), ((256, 128), F32), ((8, 256), F32), ((128, 128), F32)],
        [pltpu.VMEM((512, 2048), BF), pltpu.VMEM((2, 128), I32), DMA],
    )(group_rows, parent2)
    third = exchange(third, "dp")
    (sums,) = call(
        fine_kernel,
        32,
        [VMEM, VMEM],
        [((128, 2176), F32)],
        [pltpu.VMEM((256, 2176), BF)],
        4_000_000_000,
        4_000_000,
    )(group_rows, ids)
    third, counts = call(
        share_kernel,
        16, [VMEM, ANY], [((DP, 8, 128), F32), ((4, 128), F32)]
    )(third, sums)
    third = exchange(third, "dp")
    ready = call(
        ready_kernel,
        60,
        [SMEM] + [VMEM] * 6,
        [
            ((128, 2048), F32),
            ((128, 2048), F32),
            ((128, 128), F32),
            ((4096, 256), BF),
            ((256, 128), F32),
            ((TOP, 128), F32),
            ((256, 128), F32),
            ((2 * TOP, 256), BF),
            ((THIRD, TOP), BF),
            ((2 * MIDDLE, 256), BF),
        ],
        (),
        1_000_000_000,
        8_000_000,
    )(shrink, sums, ids, line, counts, parent2, parent3)
    (send,) = call(
        down_kernel,
        59,
        [SMEM, SMEM] + [VMEM] * 13,
        [block],
        [pltpu.VMEM((256, 128), F32), pltpu.VMEM((128, 4096), BF)],
    )(shrink, dp, third, middle, sums, *ready)
    got = exchange(send, "clus")
    fine, middle, third, spread = call(
        finish_kernel,
        16,
        [SMEM, VMEM, VMEM],
        [((256, 1024), BF), ((16, 1024), BF), ((1, 1024), BF), ((2, 128), F32)],
    )(clus, got, ready[2])
    return fine, middle, third, spread.reshape(256)


def solution(mesh):
    placed = (P(("dp", "clus"), None), P(("dp", "clus")), P(("dp", "clus")), P("dp"), P(), P())
    return jax.shard_map(
        local,
        mesh=mesh,
        in_specs=placed,
        out_specs=(
            P(("dp", "clus"), None),
            P(("dp", "clus"), None),
            P(("dp", "clus"), None),
            P(("dp", "clus")),
        ),
        check_vma=False,
    )
```

```python
import jax
import jax.numpy as jnp
from jax import lax
from jax.experimental import pallas as pl
from jax.experimental.pallas import tpu as pltpu
from jax.sharding import PartitionSpec as P

GROUPS = 16
DP = 32
FINE = 256
MIDDLE = 256
THIRD = 512
TOP = 64
WIDTH = 1024
PART = WIDTH // GROUPS
ROWS = 144
TOTAL = 131072.0
BF = jnp.bfloat16
F32 = jnp.float32
I32 = jnp.int32
MIB = 1024 * 1024


def iota(shape, dim):
    return lax.broadcasted_iota(I32, shape, dim)


def hot(mask):
    return jnp.where(mask, 1.0, 0.0).astype(BF)


def hot_row(down, row):
    return jnp.where(
        down == jnp.broadcast_to(row.astype(BF), down.shape), jnp.array(1, BF), jnp.array(0, BF)
    )


def pieces(x, count):
    out = []
    for k in range(count):
        part = x.astype(BF)
        out.append(part)
        if k + 1 < count:
            x = x - part.astype(F32)
    return out


def side(x, count):
    return jnp.concatenate(pieces(x, count), axis=1)


def turned(x):
    return pltpu.roll(x, PART, 1)


def dot(a, b):
    return jnp.dot(a, b, preferred_element_type=F32)


def dot_last(a, b):
    return lax.dot_general(a, b, (((1,), (1,)), ((), ())), preferred_element_type=F32)


def two(x):
    return x[:, 0:128] + x[:, 128:256]


def in_line(ref, first, count):
    return jnp.concatenate([ref[first + k : first + k + 1, :] for k in range(count)], axis=1)


def pack_kernel(rows_hbm, assign_hbm, parent1_hbm, send_ref, rows_ref, assign_ref, parent1_ref, sems):
    copies = [
        pltpu.make_async_copy(src, dst, sems.at[k])
        for k, (src, dst) in enumerate(
            [(rows_hbm, rows_ref), (assign_hbm, assign_ref), (parent1_hbm, parent1_ref)]
        )
    ]
    for copy in copies:
        copy.start()
    copies[1].wait()
    copies[2].wait()
    fine = assign_ref[...] & (GROUPS * FINE - 1)
    parent = parent1_ref[...] & (MIDDLE - 1)
    tile = jnp.concatenate(
        [
            (fine >> 8).astype(F32),
            (fine & (FINE - 1)).astype(F32),
            parent.astype(F32),
            jnp.zeros((10, 128), F32),
        ],
        axis=0,
    ).astype(BF)
    for k in range(GROUPS):
        send_ref[k, 128:144, :] = tile
    copies[0].wait()
    left = iota((128, 128), 1) < PART
    for g in range(GROUPS // 2):
        top = rows_ref[0:128, 128 * g : 128 * (g + 1)].astype(F32)
        low = rows_ref[128:256, 128 * g : 128 * (g + 1)].astype(F32)
        send_ref[2 * g, 0:128, :] = jnp.where(left, top, turned(low)).astype(BF)
        send_ref[2 * g + 1, 0:128, :] = jnp.where(left, turned(top), low).astype(BF)


def middle_kernel(rows_ref, parent2_hbm, third_ref, middle_ref, hot_ref, parent2_ref, sem):
    copy = pltpu.make_async_copy(parent2_hbm, parent2_ref, sem)
    copy.start()
    left = iota((256, 128), 1) < PART
    tails = [rows_ref[s, 128:144, :].astype(F32)[0:8] for s in range(GROUPS)]
    table = jnp.concatenate(
        [jnp.concatenate([tail[k : k + 1] for tail in tails], axis=0) for k in (4, 5)], axis=1
    ).astype(BF)
    down = iota((256, 256), 0).astype(F32).astype(BF)
    owner = iota((GROUPS, 256), 0).astype(F32)
    for s in range(GROUPS):
        tail = tails[s]
        high = jnp.concatenate([tail[0:1], tail[1:2]], axis=1)
        low = jnp.concatenate([tail[2:3], tail[3:4]], axis=1)
        found = dot(table, hot_row(down, low))
        parent = jnp.sum(jnp.where(owner == high, found, 0.0), axis=0, keepdims=True)
        ones = hot_row(down, parent)
        hot_ref[0:256, 128 * s : 128 * (s + 1)] = ones[:, 0:128]
        hot_ref[256:512, 128 * s : 128 * (s + 1)] = ones[:, 128:256]
    both = dot(hot_ref[...], rows_ref[:, 0:128, :].reshape(GROUPS * 128, 128))
    middle = jnp.where(left, both[0:256], both[256:512])
    middle = middle + turned(middle)
    tally = dot_last(jnp.ones((8, 2048), BF), hot_ref[0:256] + hot_ref[256:512])
    middle_ref[0:256, :] = middle
    middle_ref[256:264, :] = tally[:, 0:128]
    middle_ref[264:272, :] = tally[:, 128:256]
    copy.wait()
    line = in_line(parent2_ref, 0, 2)
    third = iota((256, 256), 0)
    first = hot(third == line)
    second = hot(third + 256 == line)
    parts = side(middle, 2)
    sums = jnp.where(left, two(dot(first, parts)), two(dot(second, parts))).reshape(DP, 8, 128)
    third_ref[:, 0] = sums[:, 0:4]
    third_ref[:, 1] = sums[:, 4:8]
    high, low = pieces(tally, 2)
    for k, ones in enumerate((first, second)):
        count = dot_last(high, ones) + dot_last(low, ones)
        for i in range(2):
            third_ref[:, 2, 2 * k + i, :] = jnp.broadcast_to(
                count[0:1, 128 * i : 128 * (i + 1)], (DP, 128)
            )


def fine_kernel(rows_ref, out_ref, ids_ref, wide_ref, acc_ref):
    lane = iota((128, 128), 1)
    left = lane < PART
    half = jnp.where(left, 0.0, 1.0)
    group = lane >> 5
    down = iota((128, 128), 0)
    for s in range(GROUPS):
        ids_ref[8 * s : 8 * s + 8, :] = rows_ref[s, 128:144, :].astype(F32)[0:8]
    columns = jnp.transpose(ids_ref[...])
    out_ref[:, 2176:2304] = columns
    for s in range(GROUPS):
        x = rows_ref[s, 0:128, :].astype(F32)
        y = turned(x)
        ones = []
        for j in range(2):
            block = slice(128 * j, 128 * (j + 1))
            twice = jnp.where(left, x, y) if j == 0 else jnp.where(left, y, x)
            low = columns[:, 8 * s + 2 + j : 8 * s + 3 + j]
            key = 2.0 * columns[:, 8 * s + j : 8 * s + j + 1] + jnp.where(low >= 128.0, 1.0, 0.0)
            key = jnp.broadcast_to(key, (128, 128))
            place = (key - half).astype(BF)
            narrow = twice.astype(BF)
            for h in range(GROUPS):
                wide_ref[block, 128 * h : 128 * (h + 1)] = jnp.where(
                    place == jnp.array(2 * h, BF), narrow, jnp.array(0, BF)
                )
            square = 0.5 * jnp.sum(twice * twice, axis=1, keepdims=True)
            hi, mid, lo = [p.astype(F32) for p in pieces(jnp.broadcast_to(square, (128, 128)), 3)]
            value = jnp.where(group == 0, hi, jnp.where(group == 1, mid, jnp.where(group == 2, lo, 1.0)))
            wide_ref[block, 2048:2176] = jnp.where(
                (lane & 31) == key.astype(I32), value, 0.0
            ).astype(BF)
            within = ids_ref[8 * s + 2 + j : 8 * s + 3 + j, :].astype(I32) & 127
            ones.append(hot(down == within))
        part = dot(jnp.concatenate(ones, axis=1), wide_ref[...])
        if s == 0:
            acc_ref[...] = part
        elif s < GROUPS - 1:
            acc_ref[...] += part
        else:
            out_ref[:, 0:2176] = acc_ref[...] + part


def share_kernel(got_ref, acc_hbm, out_ref, count_ref):
    total = got_ref[0]
    for k in range(1, DP):
        total = total + got_ref[k]
    sums = jnp.concatenate([total[0], total[1]], axis=0)
    out_ref[...] = jnp.broadcast_to(sums[None], (DP, 8, 128))
    count_ref[...] = total[2]


def ready_kernel(
    shrink_ref, acc_ref, middle_ref, third_ref, parent2_ref, parent3_ref, lines_ref, fine_cols_ref,
    cols_ref, top_inv_ref, middle_turn_ref,
):
    weight_top = shrink_ref[0] * (TOTAL / TOP)
    weight_third = shrink_ref[1] * (TOTAL / THIRD)
    weight_middle = shrink_ref[2] * (TOTAL / 8192)
    weight_fine = shrink_ref[3]
    left = iota((TOP, 128), 1) < PART
    tail = acc_ref[:, 2048:2176]
    square = tail[:, 0:32] + tail[:, 32:64] + tail[:, 64:96]
    count = tail[:, 96:128]
    lines_ref[...] = jnp.transpose(
        jnp.concatenate([square, count, jnp.zeros((128, 64), F32)], axis=1)
    )
    fine_cols_ref[...] = jnp.concatenate(
        [1.0 / (count + weight_fine), count, jnp.zeros((128, 64), F32)], axis=1
    )
    across = iota((128, 256), 1)
    third = third_ref[...]
    parent3 = parent3_ref[...].astype(F32)
    parent2 = parent2_ref[...].astype(F32)
    columns = jnp.transpose(
        jnp.concatenate(
            [
                1.0 / (third + weight_third),
                1.0 / (middle_ref[256:257, :] + weight_middle),
                1.0 / (middle_ref[264:265, :] + weight_middle),
                parent3,
                parent2,
                jnp.zeros((116, 128), F32),
            ],
            axis=0,
        )
    )
    cols_ref[...] = columns
    top_id = iota((TOP, 512), 0)
    ones = hot(top_id == in_line(parent3_ref, 0, 4))
    line = jnp.concatenate([third[k : k + 1] for k in range(4)], axis=1)
    line = jnp.broadcast_to(line, (8, 512))
    count = jnp.zeros((TOP, 8), F32)
    for part in pieces(line, 3):
        count = count + dot_last(ones, part)
    top_inv_ref[...] = jnp.broadcast_to(1.0 / (count[:, 0:1] + weight_top), (TOP, 128))
    for k in range(2):
        parent = columns[:, 10 + k : 11 + k].astype(I32)
        for b in range(2):
            middle_turn_ref[256 * b + 128 * k : 256 * b + 128 * (k + 1), :] = hot(
                across + 256 * b == parent
            )


def down_kernel(
    shrink_ref, dp_ref, got_ref, middle_ref, acc_ref, parent3_ref, lines_ref, fine_cols_ref, cols_ref,
    top_inv_ref, middle_turn_ref, send_ref, third_ref, diff_ref,
):
    left = iota((256, 128), 1) < PART
    weight_top = shrink_ref[0] * (TOTAL / TOP)
    weight_third = shrink_ref[1] * (TOTAL / THIRD)
    weight_middle = shrink_ref[2] * (TOTAL / 8192)
    weight_fine = shrink_ref[3]
    cols = cols_ref[...]
    top_id = iota((TOP, 256), 0)
    top_hot = jnp.concatenate(
        [hot(top_id == in_line(parent3_ref, 0, 2)), hot(top_id == in_line(parent3_ref, 2, 2))], axis=0
    )
    across = iota((128, TOP), 1)
    top_turn = jnp.concatenate(
        [hot(across == cols[:, 6 + k : 7 + k].astype(I32)) for k in range(4)], axis=0
    )
    third_sums = got_ref[...].reshape(256, 128)
    top = two(dot(top_hot, side(third_sums, 2)))
    top = jnp.where(left[0:TOP], top[0:TOP], top[TOP : 2 * TOP])
    top = top + turned(top)
    center = jnp.sum(top, axis=0, keepdims=True) / TOTAL
    top_means = (top + weight_top * center) * top_inv_ref[...]
    prior = two(dot(top_turn, side(top_means, 2)))
    prior = jnp.where(left, prior[0:256], prior[256:512])
    inverse = jnp.where(
        left,
        jnp.concatenate([cols[:, 0:1], cols[:, 1:2]], axis=0),
        jnp.concatenate([cols[:, 2:3], cols[:, 3:4]], axis=0),
    )
    third_means = (third_sums + weight_third * prior) * inverse
    third_ref[...] = third_means
    prior = two(dot(middle_turn_ref[...], side(third_means, 2)))
    prior = jnp.where(left, prior[0:256], prior[256:512])
    prior = prior + turned(prior)
    inverse = jnp.concatenate([cols[:, 4:5], cols[:, 5:6]], axis=0)
    middle_means = (middle_ref[0:256, :] + weight_middle * prior) * inverse
    parts = side(middle_means, 2)
    left = left[0:128]
    fine_cols = fine_cols_ref[...]
    lane = iota((128, 128), 1).astype(F32)
    lanes = (lane.astype(BF), (lane + 128.0).astype(BF))
    one, zero = jnp.array(1, BF), jnp.array(0, BF)
    for h in range(GROUPS):
        here = slice(128 * h, 128 * (h + 1))
        ones = []
        for b in range(2):
            parent = acc_ref[:, 2180 + 8 * h + b : 2181 + 8 * h + b]
            parent = jnp.broadcast_to(parent, (128, 128)).astype(BF)
            ones.append(
                jnp.concatenate([jnp.where(lane == parent, one, zero) for lane in lanes], axis=1)
            )
        found = two(dot(jnp.concatenate(ones, axis=0), parts))
        prior = jnp.where(left, found[0:128], found[128:256])
        sums = acc_ref[:, here]
        inverse = jnp.where(left, fine_cols[:, 2 * h : 2 * h + 1], fine_cols[:, 2 * h + 1 : 2 * h + 2])
        count = jnp.where(
            left, fine_cols[:, 32 + 2 * h : 33 + 2 * h], fine_cols[:, 33 + 2 * h : 34 + 2 * h]
        )
        fine = ((sums + weight_fine * prior) * inverse).astype(BF)
        send_ref[h, 0:128, :] = fine
        fine = fine.astype(F32)
        hi, lo = pieces(fine * (count * fine - 2.0 * sums), 2)
        diff_ref[:, here] = hi
        diff_ref[:, 2048 + 128 * h : 2048 + 128 * (h + 1)] = lo
    select = hot((iota((2048, 128), 0) >> 6) == iota((2048, 128), 1))
    diff = dot(diff_ref[:, 0:2048], select) + dot(diff_ref[:, 2048:4096], select)
    spread = jnp.transpose(diff)[0:32] + lines_ref[0:32]
    spread = [p.astype(F32) for p in pieces(spread, 3)]
    dp = dp_ref[0]
    own = third_ref[pl.ds(pl.multiple_of((dp % 16) * 16, 16), 16), :]
    own = jnp.where(dp < 16, own, turned(own))
    for h in range(GROUPS):
        send_ref[h, 128:144, :] = jnp.concatenate(
            [
                jnp.where(
                    left[0:8], middle_means[16 * h : 16 * h + 8], middle_means[16 * h + 8 : 16 * h + 16]
                ),
                own[h : h + 1],
                spread[0][2 * h : 2 * h + 2],
                spread[1][2 * h : 2 * h + 2],
                spread[2][2 * h : 2 * h + 2],
                jnp.zeros((1, 128), F32),
            ],
            axis=0,
        ).astype(BF)


def finish_kernel(clus_ref, got_ref, lines_ref, out_ref, middle_ref, third_ref, spread_ref):
    left = iota((128, 128), 1) < PART
    total = jnp.zeros((8, 128), F32)
    for g in range(GROUPS // 2):
        here = slice(128 * g, 128 * (g + 1))
        a = got_ref[2 * g, 0:128, :].astype(F32)
        b = got_ref[2 * g + 1, 0:128, :].astype(F32)
        out_ref[0:128, here] = jnp.where(left, a, turned(b)).astype(BF)
        out_ref[128:256, here] = jnp.where(left, turned(a), b).astype(BF)
        a = got_ref[2 * g, 128:144, :].astype(F32)
        b = got_ref[2 * g + 1, 128:144, :].astype(F32)
        first = jnp.where(left[0:16], a, turned(b))
        second = jnp.where(left[0:16], turned(a), b)
        middle_ref[:, here] = jnp.concatenate([first[0:8], second[0:8]], axis=0).astype(BF)
        third_ref[:, here] = first[8:9].astype(BF)
        total = total + a[8:16] + b[8:16]
    total = total[1:3] + total[3:5] + total[5:7]
    row = iota((32, 128), 0)
    counts = [
        jnp.sum(jnp.where(row == 2 * clus_ref[0] + b, lines_ref[32:64], 0.0), axis=0, keepdims=True)
        for b in range(2)
    ]
    spread_ref[...] = total / (WIDTH * (jnp.concatenate(counts, axis=0) + 1.0))


VMEM = pl.BlockSpec(memory_space=pltpu.VMEM)
SMEM = pl.BlockSpec(memory_space=pltpu.SMEM)
ANY = pl.BlockSpec(memory_space=pl.ANY)
DMA = pltpu.SemaphoreType.DMA


def call(kernel, limit, ins, outs, scratch=(), flops=0, moved=0):
    return pl.pallas_call(
        kernel,
        out_shape=[jax.ShapeDtypeStruct(s, d) for s, d in outs],
        in_specs=ins,
        out_specs=[VMEM] * len(outs),
        scratch_shapes=list(scratch),
        compiler_params=pltpu.CompilerParams(vmem_limit_bytes=limit * MIB),
        cost_estimate=pl.CostEstimate(flops=flops, bytes_accessed=moved, transcendentals=0),
    )


def exchange(x, axis):
    return lax.all_to_all(x, axis, split_axis=0, concat_axis=0, tiled=True)


def local(rows, fine_assign, parent1, parent2, parent3, shrink):
    dp = lax.axis_index("dp").astype(I32).reshape(1)
    clus = lax.axis_index("clus").astype(I32).reshape(1)
    parent2 = parent2.reshape(2, 128)
    parent3 = parent3.reshape(4, 128)
    block = ((GROUPS, ROWS, 128), BF)
    (send,) = call(
        pack_kernel,
        60,
        [ANY] * 3,
        [block],
        [
            pltpu.VMEM((256, WIDTH), BF),
            pltpu.VMEM((2, 128), I32),
            pltpu.VMEM((2, 128), I32),
            DMA((3,)),
        ],
    )(rows, fine_assign.reshape(2, 128), parent1.reshape(2, 128))
    group_rows = exchange(send, "clus")
    third, middle = call(
        middle_kernel,
        32,
        [VMEM, ANY],
        [((DP, 3, 4, 128), F32), ((272, 128), F32)],
        [pltpu.VMEM((512, 2048), BF), pltpu.VMEM((2, 128), I32), DMA],
    )(group_rows, parent2)
    third = exchange(third, "dp")
    (sums,) = call(
        fine_kernel,
        32,
        [VMEM],
        [((128, 2304), F32)],
        [pltpu.VMEM((128, 128), F32), pltpu.VMEM((256, 2176), BF), pltpu.VMEM((128, 2176), F32)],
        4_000_000_000,
        4_000_000,
    )(group_rows)
    third, counts = call(
        share_kernel,
        16, [VMEM, ANY], [((DP, 8, 128), F32), ((4, 128), F32)]
    )(third, sums)
    third = exchange(third, "dp")
    ready = call(
        ready_kernel,
        24,
        [SMEM] + [VMEM] * 5,
        [
            ((128, 128), F32),
            ((128, 128), F32),
            ((128, 128), F32),
            ((TOP, 128), F32),
            ((2 * MIDDLE, 256), BF),
        ],
        (),
        1_000_000_000,
        8_000_000,
    )(shrink, sums, middle, counts, parent2, parent3)
    (send,) = call(
        down_kernel,
        24,
        [SMEM, SMEM] + [VMEM] * 9,
        [block],
        [pltpu.VMEM((256, 128), F32), pltpu.VMEM((128, 4096), BF)],
    )(shrink, dp, third, middle, sums, parent3, *ready)
    got = exchange(send, "clus")
    fine, middle, third, spread = call(
        finish_kernel,
        16,
        [SMEM, VMEM, VMEM],
        [((256, 1024), BF), ((16, 1024), BF), ((1, 1024), BF), ((2, 128), F32)],
    )(clus, got, ready[0])
    return fine, middle, third, spread.reshape(256)


def solution(mesh):
    placed = (P(("dp", "clus"), None), P(("dp", "clus")), P(("dp", "clus")), P("dp"), P(), P())
    return jax.shard_map(
        local,
        mesh=mesh,
        in_specs=placed,
        out_specs=(
            P(("dp", "clus"), None),
            P(("dp", "clus"), None),
            P(("dp", "clus"), None),
            P(("dp", "clus")),
        ),
        check_vma=False,
    )
```

```python
import jax
import jax.numpy as jnp
from jax import lax
from jax.experimental import pallas as pl
from jax.experimental.pallas import tpu as pltpu
from jax.sharding import PartitionSpec as P

GROUPS = 16
DP = 32
FINE = 256
MIDDLE = 256
THIRD = 512
TOP = 64
WIDTH = 1024
PART = WIDTH // GROUPS
ROWS = 144
TOTAL = 131072.0
BF = jnp.bfloat16
F32 = jnp.float32
I32 = jnp.int32
MIB = 1024 * 1024


def iota(shape, dim):
    return lax.broadcasted_iota(I32, shape, dim)


def hot(mask):
    return jnp.where(mask, 1.0, 0.0).astype(BF)


def hot_row(down, row):
    return jnp.where(
        down == jnp.broadcast_to(row.astype(BF), down.shape), jnp.array(1, BF), jnp.array(0, BF)
    )


def pieces(x, count):
    out = []
    for k in range(count):
        part = x.astype(BF)
        out.append(part)
        if k + 1 < count:
            x = x - part.astype(F32)
    return out


def side(x, count):
    return jnp.concatenate(pieces(x, count), axis=1)


def turned(x):
    return pltpu.roll(x, PART, 1)


def dot(a, b):
    return jnp.dot(a, b, preferred_element_type=F32)


def dot_last(a, b):
    return lax.dot_general(a, b, (((1,), (1,)), ((), ())), preferred_element_type=F32)


def two(x):
    return x[:, 0:128] + x[:, 128:256]


def in_line(ref, first, count):
    return jnp.concatenate([ref[first + k : first + k + 1, :] for k in range(count)], axis=1)


def pack_kernel(rows_ref, assign_ref, parent1_ref, send_ref):
    fine = assign_ref[...] & (GROUPS * FINE - 1)
    parent = parent1_ref[...] & (MIDDLE - 1)
    tile = jnp.concatenate(
        [
            (fine >> 8).astype(F32),
            (fine & (FINE - 1)).astype(F32),
            parent.astype(F32),
            jnp.zeros((10, 128), F32),
        ],
        axis=0,
    ).astype(BF)
    left = iota((128, 128), 1) < PART
    for g in range(GROUPS // 2):
        top = rows_ref[0:128, 128 * g : 128 * (g + 1)].astype(F32)
        low = rows_ref[128:256, 128 * g : 128 * (g + 1)].astype(F32)
        send_ref[2 * g, 0:128, :] = jnp.where(left, top, turned(low)).astype(BF)
        send_ref[2 * g + 1, 0:128, :] = jnp.where(left, turned(top), low).astype(BF)
        send_ref[2 * g, 128:144, :] = tile
        send_ref[2 * g + 1, 128:144, :] = tile


def middle_kernel(rows_ref, parent2_hbm, third_ref, middle_ref, hot_ref, parent2_ref, sem):
    copy = pltpu.make_async_copy(parent2_hbm, parent2_ref, sem)
    copy.start()
    left = iota((256, 128), 1) < PART
    tails = [rows_ref[s, 128:144, :].astype(F32)[0:8] for s in range(GROUPS)]
    table = jnp.concatenate(
        [jnp.concatenate([tail[k : k + 1] for tail in tails], axis=0) for k in (4, 5)], axis=1
    ).astype(BF)
    down = iota((256, 256), 0).astype(F32).astype(BF)
    owner = iota((GROUPS, 256), 0).astype(F32)
    for s in range(GROUPS):
        tail = tails[s]
        high = jnp.concatenate([tail[0:1], tail[1:2]], axis=1)
        low = jnp.concatenate([tail[2:3], tail[3:4]], axis=1)
        found = dot(table, hot_row(down, low))
        parent = jnp.sum(jnp.where(owner == high, found, 0.0), axis=0, keepdims=True)
        ones = hot_row(down, parent)
        hot_ref[0:256, 128 * s : 128 * (s + 1)] = ones[:, 0:128]
        hot_ref[256:512, 128 * s : 128 * (s + 1)] = ones[:, 128:256]
    both = dot(hot_ref[...], rows_ref[:, 0:128, :].reshape(GROUPS * 128, 128))
    middle = jnp.where(left, both[0:256], both[256:512])
    middle = middle + turned(middle)
    tally = dot_last(jnp.ones((8, 2048), BF), hot_ref[0:256] + hot_ref[256:512])
    middle_ref[0:256, :] = middle
    middle_ref[256:264, :] = tally[:, 0:128]
    middle_ref[264:272, :] = tally[:, 128:256]
    copy.wait()
    line = in_line(parent2_ref, 0, 2)
    third = iota((256, 256), 0)
    first = hot(third == line)
    second = hot(third + 256 == line)
    parts = side(middle, 2)
    sums = jnp.where(left, two(dot(first, parts)), two(dot(second, parts))).reshape(DP, 8, 128)
    third_ref[:, 0] = sums[:, 0:4]
    third_ref[:, 1] = sums[:, 4:8]
    high, low = pieces(tally, 2)
    for k, ones in enumerate((first, second)):
        count = dot_last(high, ones) + dot_last(low, ones)
        for i in range(2):
            third_ref[:, 2, 2 * k + i, :] = jnp.broadcast_to(
                count[0:1, 128 * i : 128 * (i + 1)], (DP, 128)
            )


def fine_kernel(rows_ref, out_ref, ids_ref, wide_ref, acc_ref):
    lane = iota((128, 128), 1)
    left = lane < PART
    half = jnp.where(left, 0.0, 1.0)
    group = lane >> 5
    down = iota((128, 128), 0)
    for s in range(GROUPS):
        ids_ref[8 * s : 8 * s + 8, :] = rows_ref[s, 128:144, :].astype(F32)[0:8]
    columns = jnp.transpose(ids_ref[...])
    out_ref[:, 2176:2304] = columns
    for s in range(GROUPS):
        x = rows_ref[s, 0:128, :].astype(F32)
        y = turned(x)
        ones = []
        for j in range(2):
            block = slice(128 * j, 128 * (j + 1))
            twice = jnp.where(left, x, y) if j == 0 else jnp.where(left, y, x)
            low = columns[:, 8 * s + 2 + j : 8 * s + 3 + j]
            key = 2.0 * columns[:, 8 * s + j : 8 * s + j + 1] + jnp.where(low >= 128.0, 1.0, 0.0)
            key = jnp.broadcast_to(key, (128, 128))
            place = (key - half).astype(BF)
            narrow = twice.astype(BF)
            for h in range(GROUPS):
                wide_ref[block, 128 * h : 128 * (h + 1)] = jnp.where(
                    place == jnp.array(2 * h, BF), narrow, jnp.array(0, BF)
                )
            square = 0.5 * jnp.sum(twice * twice, axis=1, keepdims=True)
            hi, mid, lo = [p.astype(F32) for p in pieces(jnp.broadcast_to(square, (128, 128)), 3)]
            value = jnp.where(group == 0, hi, jnp.where(group == 1, mid, jnp.where(group == 2, lo, 1.0)))
            wide_ref[block, 2048:2176] = jnp.where(
                (lane & 31) == key.astype(I32), value, 0.0
            ).astype(BF)
            within = ids_ref[8 * s + 2 + j : 8 * s + 3 + j, :].astype(I32) & 127
            ones.append(hot(down == within))
        part = dot(jnp.concatenate(ones, axis=1), wide_ref[...])
        if s == 0:
            acc_ref[...] = part
        elif s < GROUPS - 1:
            acc_ref[...] += part
        else:
            out_ref[:, 0:2176] = acc_ref[...] + part


def share_kernel(got_ref, acc_hbm, out_ref, count_ref):
    total = got_ref[0]
    for k in range(1, DP):
        total = total + got_ref[k]
    sums = jnp.concatenate([total[0], total[1]], axis=0)
    out_ref[...] = jnp.broadcast_to(sums[None], (DP, 8, 128))
    count_ref[...] = total[2]


def ready_kernel(
    index_ref, shrink_ref, acc_ref, middle_ref, third_ref, parent2_ref, parent3_ref, inv_ref, lines_ref, cols_ref,
    middle_turn_ref, top_turn_ref, third_inv_ref, top_inv_ref, down_ref, scale_ref, own_ref,
):
    weight_third = shrink_ref[1] * (TOTAL / THIRD)
    weight_middle = shrink_ref[2] * (TOTAL / 8192)
    left = iota((128, 128), 1) < PART
    tail = acc_ref[:, 2048:2176]
    square = tail[:, 0:32] + tail[:, 32:64] + tail[:, 64:96]
    count = tail[:, 96:128]
    lines = jnp.transpose(jnp.concatenate([square, count, jnp.zeros((128, 64), F32)], axis=1))
    lines_ref[...] = lines[0:64]
    row = iota((32, 128), 0)
    own = [
        jnp.sum(jnp.where(row == 2 * index_ref[1] + b, lines[32:64], 0.0), axis=0, keepdims=True)
        for b in range(2)
    ]
    own_ref[...] = jnp.concatenate(own + [jnp.zeros((6, 128), F32)], axis=0)
    inverse = 1.0 / (count + shrink_ref[3])
    for h in range(GROUPS):
        inv_ref[:, 128 * h : 128 * (h + 1)] = jnp.where(
            left, inverse[:, 2 * h : 2 * h + 1], inverse[:, 2 * h + 1 : 2 * h + 2]
        )
    third = third_ref[...]
    cols = jnp.transpose(
        jnp.concatenate(
            [
                1.0 / (middle_ref[256:257, :] + weight_middle),
                1.0 / (middle_ref[264:265, :] + weight_middle),
                parent3_ref[...].astype(F32),
                parent2_ref[...].astype(F32),
                1.0 / (third + weight_third),
                jnp.zeros((116, 128), F32),
            ],
            axis=0,
        )
    )
    third_inv_ref[...] = jnp.concatenate(
        [jnp.where(left, cols[:, 8 + k : 9 + k], cols[:, 10 + k : 11 + k]) for k in range(2)], axis=0
    )
    across = iota((128, 256), 1)
    for k in range(2):
        parent = cols[:, 6 + k : 7 + k].astype(I32)
        for b in range(2):
            middle_turn_ref[256 * b + 128 * k : 256 * b + 128 * (k + 1), :] = hot(
                across + 256 * b == parent
            )
    for k in range(4):
        top_turn_ref[128 * k : 128 * (k + 1), :] = hot(
            across[:, 0:128] == cols[:, 2 + k : 3 + k].astype(I32)
        )
    down = jnp.zeros((256, 128), F32)
    scale = jnp.zeros((256, 128), F32)
    for b in range(2):
        turn = middle_turn_ref[256 * b : 256 * (b + 1), :]
        down = down + dot(turn, top_turn_ref[256 * b : 256 * (b + 1), :])
        column = jnp.concatenate([cols[:, 8 + 2 * b + k : 9 + 2 * b + k] for k in range(2)], axis=0)
        for part in pieces(jnp.broadcast_to(weight_third * column, (256, 128)), 3):
            scale = scale + dot(turn, part)
    down_ref[...] = down.astype(BF)
    scale_ref[...] = scale
    ones = hot(iota((TOP, 512), 0) == in_line(parent3_ref, 0, 4))
    line = jnp.concatenate([third[k : k + 1] for k in range(4)], axis=1)
    parts = pieces(jnp.broadcast_to(line, (8, 512)), 3)
    count = dot_last(ones, parts[0]) + dot_last(ones, parts[1]) + dot_last(ones, parts[2])
    top_inv_ref[...] = jnp.broadcast_to(
        1.0 / (count[:, 0:1] + shrink_ref[0] * (TOTAL / TOP)), (TOP, 128)
    )
    cols_ref[...] = cols


def down_kernel(
    index_ref, shrink_ref, got_ref, middle_ref, parent3_ref, acc_ref, inv_ref, lines_ref, cols_ref, middle_turn_ref,
    top_turn_ref, third_inv_ref, top_inv_ref, down_ref, scale_ref, send_ref,
):
    left = iota((256, 128), 1) < PART
    weight_top = shrink_ref[0] * (TOTAL / TOP)
    weight_third = shrink_ref[1] * (TOTAL / THIRD)
    weight_middle = shrink_ref[2] * (TOTAL / 8192)
    weight_fine = shrink_ref[3]
    cols = cols_ref[...]
    top_id = iota((TOP, 256), 0)
    top_hot = jnp.concatenate(
        [hot(top_id == in_line(parent3_ref, 0, 2)), hot(top_id == in_line(parent3_ref, 2, 2))], axis=0
    )
    third_sums = got_ref[...].reshape(256, 128)
    top = two(dot(top_hot, side(third_sums, 2)))
    top = jnp.where(left[0:TOP], top[0:TOP], top[TOP : 2 * TOP])
    top = top + turned(top)
    center = jnp.sum(top, axis=0, keepdims=True) / TOTAL
    top_means = (top + weight_top * center) * top_inv_ref[...]
    term = two(dot(middle_turn_ref[...], side(third_sums * third_inv_ref[...], 2)))
    term = jnp.where(left, term[0:256], term[256:512])
    parts = side(top_means, 2)
    prior = term + turned(term) + scale_ref[...] * two(dot(down_ref[:, 0:TOP], parts))
    index = index_ref[0]
    rows = pl.ds(pl.multiple_of((index % 16) * 16, 16), 16)
    own = two(dot(top_turn_ref[pl.ds(pl.multiple_of(index * 16, 16), 16), 0:TOP], parts))
    own = (got_ref[pl.ds((index % 16) * 2, 2)].reshape(16, 128) + weight_third * own) * third_inv_ref[rows, :]
    own = jnp.where(index < 16, own, turned(own))
    inverse = jnp.concatenate([cols[:, 0:1], cols[:, 1:2]], axis=0)
    middle_means = (middle_ref[0:256, :] + weight_middle * prior) * inverse
    parts = side(middle_means, 2)
    left = left[0:128]
    lane = iota((128, 128), 1).astype(F32)
    lanes = (lane.astype(BF), (lane + 128.0).astype(BF))
    one, zero = jnp.array(1, BF), jnp.array(0, BF)
    halves = hot((iota((16, 256), 1) & 127) >> 6 == iota((16, 256), 0))
    for h in range(GROUPS):
        here = slice(128 * h, 128 * (h + 1))
        ones = []
        for b in range(2):
            parent = acc_ref[:, 2180 + 8 * h + b : 2181 + 8 * h + b]
            parent = jnp.broadcast_to(parent, (128, 128)).astype(BF)
            ones.append(
                jnp.concatenate([jnp.where(lane == parent, one, zero) for lane in lanes], axis=1)
            )
        found = two(dot(jnp.concatenate(ones, axis=0), parts))
        prior = jnp.where(left, found[0:128], found[128:256])
        sums = acc_ref[:, here]
        fine = ((sums + weight_fine * prior) * inv_ref[:, here]).astype(BF)
        send_ref[h, 0:128, :] = fine
        fine = fine.astype(F32)
        spread = (
            lines_ref[2 * h : 2 * h + 2]
            + lines_ref[32 + 2 * h : 34 + 2 * h] * dot_last(halves, side(fine * fine, 2))[0:2]
            - 2.0 * dot_last(halves, side(fine * sums, 2))[0:2]
        )
        send_ref[h, 128:144, :] = jnp.concatenate(
            [
                jnp.where(
                    left[0:8], middle_means[16 * h : 16 * h + 8], middle_means[16 * h + 8 : 16 * h + 16]
                ),
                own[h : h + 1],
            ]
            + [part.astype(F32) for part in pieces(spread, 3)]
            + [jnp.zeros((1, 128), F32)],
            axis=0,
        ).astype(BF)


def finish_kernel(got_ref, own_ref, out_ref, middle_ref, third_ref, spread_ref):
    left = iota((128, 128), 1) < PART
    total = jnp.zeros((8, 128), F32)
    for g in range(GROUPS // 2):
        here = slice(128 * g, 128 * (g + 1))
        a = got_ref[2 * g, 0:128, :].astype(F32)
        b = got_ref[2 * g + 1, 0:128, :].astype(F32)
        out_ref[0:128, here] = jnp.where(left, a, turned(b)).astype(BF)
        out_ref[128:256, here] = jnp.where(left, turned(a), b).astype(BF)
        a = got_ref[2 * g, 128:144, :].astype(F32)
        b = got_ref[2 * g + 1, 128:144, :].astype(F32)
        first = jnp.where(left[0:16], a, turned(b))
        second = jnp.where(left[0:16], turned(a), b)
        middle_ref[:, here] = jnp.concatenate([first[0:8], second[0:8]], axis=0).astype(BF)
        third_ref[:, here] = first[8:9].astype(BF)
        total = total + a[8:16] + b[8:16]
    total = total[1:3] + total[3:5] + total[5:7]
    spread_ref[...] = total / (WIDTH * (own_ref[0:2] + 1.0))


VMEM = pl.BlockSpec(memory_space=pltpu.VMEM)
SMEM = pl.BlockSpec(memory_space=pltpu.SMEM)
ANY = pl.BlockSpec(memory_space=pl.ANY)
DMA = pltpu.SemaphoreType.DMA


def call(kernel, limit, ins, outs, scratch=(), flops=0, moved=0):
    return pl.pallas_call(
        kernel,
        out_shape=[jax.ShapeDtypeStruct(s, d) for s, d in outs],
        in_specs=ins,
        out_specs=[VMEM] * len(outs),
        scratch_shapes=list(scratch),
        compiler_params=pltpu.CompilerParams(vmem_limit_bytes=limit * MIB),
        cost_estimate=pl.CostEstimate(flops=flops, bytes_accessed=moved, transcendentals=0),
    )


def exchange(x, axis):
    return lax.all_to_all(x, axis, split_axis=0, concat_axis=0, tiled=True)


def local(rows, fine_assign, parent1, parent2, parent3, shrink):
    index = jnp.stack([lax.axis_index("dp"), lax.axis_index("clus")]).astype(I32)
    parent2 = parent2.reshape(2, 128)
    parent3 = parent3.reshape(4, 128)
    block = ((GROUPS, ROWS, 128), BF)
    (send,) = call(pack_kernel, 60, [VMEM] * 3, [block])(
        rows, fine_assign.reshape(2, 128), parent1.reshape(2, 128)
    )
    group_rows = exchange(send, "clus")
    third, middle = call(
        middle_kernel,
        24,
        [VMEM, ANY],
        [((DP, 3, 4, 128), F32), ((272, 128), F32)],
        [pltpu.VMEM((512, 2048), BF), pltpu.VMEM((2, 128), I32), DMA],
    )(group_rows, parent2)
    third = exchange(third, "dp")
    (sums,) = call(
        fine_kernel,
        24,
        [VMEM],
        [((128, 2304), F32)],
        [pltpu.VMEM((128, 128), F32), pltpu.VMEM((256, 2176), BF), pltpu.VMEM((128, 2176), F32)],
        4_000_000_000,
        4_000_000,
    )(group_rows)
    third, counts = call(share_kernel, 24, [VMEM, ANY], [((DP, 8, 128), F32), ((4, 128), F32)])(
        third, sums
    )
    third = exchange(third, "dp")
    *ready, own = call(
        ready_kernel,
        24,
        [SMEM, SMEM] + [VMEM] * 5,
        [
            ((128, 2048), F32),
            ((64, 128), F32),
            ((128, 128), F32),
            ((2 * MIDDLE, 256), BF),
            ((THIRD, 128), BF),
            ((256, 128), F32),
            ((TOP, 128), F32),
            ((256, 128), BF),
            ((256, 128), F32),
            ((8, 128), F32),
        ],
        (),
        1_000_000_000,
        8_000_000,
    )(index, shrink, sums, middle, counts, parent2, parent3)
    (send,) = call(down_kernel, 24, [SMEM, SMEM] + [VMEM] * 13, [block])(index, shrink, third, middle, parent3, sums, *ready)
    got = exchange(send, "clus")
    fine, middle, third, spread = call(
        finish_kernel,
        24,
        [VMEM, VMEM],
        [((256, 1024), BF), ((16, 1024), BF), ((1, 1024), BF), ((2, 128), F32)],
    )(got, own)
    return fine, middle, third, spread.reshape(256)


def solution(mesh):
    placed = (P(("dp", "clus"), None), P(("dp", "clus")), P(("dp", "clus")), P("dp"), P(), P())
    return jax.shard_map(
        local,
        mesh=mesh,
        in_specs=placed,
        out_specs=(
            P(("dp", "clus"), None),
            P(("dp", "clus"), None),
            P(("dp", "clus"), None),
            P(("dp", "clus")),
        ),
        check_vma=False,
    )
```

```python
import jax
import jax.numpy as jnp
from jax import lax
from jax.experimental import pallas as pl
from jax.experimental.pallas import tpu as pltpu
from jax.sharding import PartitionSpec as P

GROUPS = 16
DP = 32
FINE = 256
MIDDLE = 256
THIRD = 512
TOP = 64
WIDTH = 1024
PART = WIDTH // GROUPS
ROWS = 144
TOTAL = 131072.0
BF = jnp.bfloat16
F32 = jnp.float32
I32 = jnp.int32
MIB = 1024 * 1024


def iota(shape, dim):
    return lax.broadcasted_iota(I32, shape, dim)


def hot(mask):
    return jnp.where(mask, 1.0, 0.0).astype(BF)


def hot_row(down, row):
    return jnp.where(
        down == jnp.broadcast_to(row.astype(BF), down.shape), jnp.array(1, BF), jnp.array(0, BF)
    )


def pieces(x, count):
    out = []
    for k in range(count):
        part = x.astype(BF)
        out.append(part)
        if k + 1 < count:
            x = x - part.astype(F32)
    return out


def side(x, count):
    return jnp.concatenate(pieces(x, count), axis=1)


def turned(x):
    return pltpu.roll(x, PART, 1)


def dot(a, b):
    return jnp.dot(a, b, preferred_element_type=F32)


def dot_last(a, b):
    return lax.dot_general(a, b, (((1,), (1,)), ((), ())), preferred_element_type=F32)


def two(x):
    return x[:, 0:128] + x[:, 128:256]


def in_line(ref, first, count):
    return jnp.concatenate([ref[first + k : first + k + 1, :] for k in range(count)], axis=1)


def pack_kernel(rows_ref, assign_ref, parent1_ref, send_ref):
    fine = assign_ref[...] & (GROUPS * FINE - 1)
    parent = parent1_ref[...] & (MIDDLE - 1)
    tile = jnp.concatenate(
        [
            (fine >> 8).astype(F32),
            (fine & (FINE - 1)).astype(F32),
            parent.astype(F32),
            jnp.zeros((10, 128), F32),
        ],
        axis=0,
    ).astype(BF)
    left = iota((128, 128), 1) < PART
    for g in range(GROUPS // 2):
        top = rows_ref[0:128, 128 * g : 128 * (g + 1)].astype(F32)
        low = rows_ref[128:256, 128 * g : 128 * (g + 1)].astype(F32)
        send_ref[2 * g, 0:128, :] = jnp.where(left, top, turned(low)).astype(BF)
        send_ref[2 * g + 1, 0:128, :] = jnp.where(left, turned(top), low).astype(BF)
        send_ref[2 * g, 128:144, :] = tile
        send_ref[2 * g + 1, 128:144, :] = tile


def middle_kernel(rows_ref, parent2_hbm, third_ref, middle_ref, hot_ref, parent2_ref, sem):
    copy = pltpu.make_async_copy(parent2_hbm, parent2_ref, sem)
    copy.start()
    left = iota((256, 128), 1) < PART
    tails = [rows_ref[s, 128:144, :].astype(F32)[0:8] for s in range(GROUPS)]
    table = jnp.concatenate(
        [jnp.concatenate([tail[k : k + 1] for tail in tails], axis=0) for k in (4, 5)], axis=1
    ).astype(BF)
    down = iota((256, 256), 0).astype(F32).astype(BF)
    owner = iota((GROUPS, 256), 0).astype(F32)
    for s in range(GROUPS):
        tail = tails[s]
        high = jnp.concatenate([tail[0:1], tail[1:2]], axis=1)
        low = jnp.concatenate([tail[2:3], tail[3:4]], axis=1)
        found = dot(table, hot_row(down, low))
        parent = jnp.sum(jnp.where(owner == high, found, 0.0), axis=0, keepdims=True)
        ones = hot_row(down, parent)
        hot_ref[0:256, 128 * s : 128 * (s + 1)] = ones[:, 0:128]
        hot_ref[256:512, 128 * s : 128 * (s + 1)] = ones[:, 128:256]
    both = dot(hot_ref[...], rows_ref[:, 0:128, :].reshape(GROUPS * 128, 128))
    middle = jnp.where(left, both[0:256], both[256:512])
    middle = middle + turned(middle)
    tally = dot_last(jnp.ones((8, 2048), BF), hot_ref[0:256] + hot_ref[256:512])
    middle_ref[0:256, :] = middle
    middle_ref[256:264, :] = tally[:, 0:128]
    middle_ref[264:272, :] = tally[:, 128:256]
    copy.wait()
    line = in_line(parent2_ref, 0, 2)
    third = iota((256, 256), 0)
    first = hot(third == line)
    second = hot(third + 256 == line)
    parts = side(middle, 2)
    sums = jnp.where(left, two(dot(first, parts)), two(dot(second, parts))).reshape(DP, 8, 128)
    high, low = pieces(tally, 2)
    counts = [dot_last(high, ones) + dot_last(low, ones) for ones in (first, second)]
    counts = jnp.concatenate(
        [count[0:1, 128 * i : 128 * (i + 1)] for count in counts for i in range(2)], axis=0
    )
    tail = jnp.concatenate([part.astype(F32) for part in pieces(counts, 2)], axis=0)
    tail = jnp.broadcast_to(tail[None], (DP, 8, 128))
    third_ref[...] = jnp.concatenate([sums, tail], axis=1).astype(BF)


def fine_kernel(rows_ref, out_ref, ids_ref, wide_ref, acc_ref):
    lane = iota((128, 128), 1)
    left = lane < PART
    half = jnp.where(left, 0.0, 1.0)
    group = lane >> 5
    down = iota((128, 128), 0)
    for s in range(GROUPS):
        ids_ref[8 * s : 8 * s + 8, :] = rows_ref[s, 128:144, :].astype(F32)[0:8]
    columns = jnp.transpose(ids_ref[...])
    out_ref[:, 2176:2304] = columns
    for s in range(GROUPS):
        x = rows_ref[s, 0:128, :].astype(F32)
        y = turned(x)
        ones = []
        for j in range(2):
            block = slice(128 * j, 128 * (j + 1))
            twice = jnp.where(left, x, y) if j == 0 else jnp.where(left, y, x)
            low = columns[:, 8 * s + 2 + j : 8 * s + 3 + j]
            key = 2.0 * columns[:, 8 * s + j : 8 * s + j + 1] + jnp.where(low >= 128.0, 1.0, 0.0)
            key = jnp.broadcast_to(key, (128, 128))
            place = (key - half).astype(BF)
            narrow = twice.astype(BF)
            for h in range(GROUPS):
                wide_ref[block, 128 * h : 128 * (h + 1)] = jnp.where(
                    place == jnp.array(2 * h, BF), narrow, jnp.array(0, BF)
                )
            square = 0.5 * jnp.sum(twice * twice, axis=1, keepdims=True)
            hi, mid, lo = [p.astype(F32) for p in pieces(jnp.broadcast_to(square, (128, 128)), 3)]
            value = jnp.where(group == 0, hi, jnp.where(group == 1, mid, jnp.where(group == 2, lo, 1.0)))
            wide_ref[block, 2048:2176] = jnp.where(
                (lane & 31) == key.astype(I32), value, 0.0
            ).astype(BF)
            within = ids_ref[8 * s + 2 + j : 8 * s + 3 + j, :].astype(I32) & 127
            ones.append(hot(down == within))
        part = dot(jnp.concatenate(ones, axis=1), wide_ref[...])
        if s == 0:
            acc_ref[...] = part
        elif s < GROUPS - 1:
            acc_ref[...] += part
        else:
            out_ref[:, 0:2176] = acc_ref[...] + part


def share_kernel(got_ref, acc_hbm, out_ref, count_ref):
    total = got_ref[0].astype(F32)
    for k in range(1, DP):
        total = total + got_ref[k].astype(F32)
    out_ref[...] = jnp.broadcast_to(total[None, 0:8], (DP, 8, 128))
    count_ref[...] = total[8:12] + total[12:16]


def ready_kernel(
    index_ref, shrink_ref, acc_ref, middle_ref, third_ref, parent2_ref, parent3_ref, inv_ref, lines_ref, cols_ref,
    middle_turn_ref, top_turn_ref, third_inv_ref, top_inv_ref, down_ref, scale_ref, own_ref,
):
    weight_third = shrink_ref[1] * (TOTAL / THIRD)
    weight_middle = shrink_ref[2] * (TOTAL / 8192)
    left = iota((128, 128), 1) < PART
    tail = acc_ref[:, 2048:2176]
    square = tail[:, 0:32] + tail[:, 32:64] + tail[:, 64:96]
    count = tail[:, 96:128]
    lines = jnp.transpose(jnp.concatenate([square, count, jnp.zeros((128, 64), F32)], axis=1))
    lines_ref[...] = lines[0:64]
    row = iota((32, 128), 0)
    own = [
        jnp.sum(jnp.where(row == 2 * index_ref[1] + b, lines[32:64], 0.0), axis=0, keepdims=True)
        for b in range(2)
    ]
    own_ref[...] = jnp.concatenate(own + [jnp.zeros((6, 128), F32)], axis=0)
    inverse = 1.0 / (count + shrink_ref[3])
    for h in range(GROUPS):
        inv_ref[:, 128 * h : 128 * (h + 1)] = jnp.where(
            left, inverse[:, 2 * h : 2 * h + 1], inverse[:, 2 * h + 1 : 2 * h + 2]
        )
    third = third_ref[...]
    cols = jnp.transpose(
        jnp.concatenate(
            [
                1.0 / (middle_ref[256:257, :] + weight_middle),
                1.0 / (middle_ref[264:265, :] + weight_middle),
                parent3_ref[...].astype(F32),
                parent2_ref[...].astype(F32),
                1.0 / (third + weight_third),
                jnp.zeros((116, 128), F32),
            ],
            axis=0,
        )
    )
    third_inv_ref[...] = jnp.concatenate(
        [jnp.where(left, cols[:, 8 + k : 9 + k], cols[:, 10 + k : 11 + k]) for k in range(2)], axis=0
    )
    across = iota((128, 256), 1)
    for k in range(2):
        parent = cols[:, 6 + k : 7 + k].astype(I32)
        for b in range(2):
            middle_turn_ref[256 * b + 128 * k : 256 * b + 128 * (k + 1), :] = hot(
                across + 256 * b == parent
            )
    for k in range(4):
        top_turn_ref[128 * k : 128 * (k + 1), :] = hot(
            across[:, 0:128] == cols[:, 2 + k : 3 + k].astype(I32)
        )
    down = jnp.zeros((256, 128), F32)
    scale = jnp.zeros((256, 128), F32)
    for b in range(2):
        turn = middle_turn_ref[256 * b : 256 * (b + 1), :]
        down = down + dot(turn, top_turn_ref[256 * b : 256 * (b + 1), :])
        column = jnp.concatenate([cols[:, 8 + 2 * b + k : 9 + 2 * b + k] for k in range(2)], axis=0)
        for part in pieces(jnp.broadcast_to(weight_third * column, (256, 128)), 3):
            scale = scale + dot(turn, part)
    down_ref[...] = down.astype(BF)
    scale_ref[...] = scale
    ones = hot(iota((TOP, 512), 0) == in_line(parent3_ref, 0, 4))
    line = jnp.concatenate([third[k : k + 1] for k in range(4)], axis=1)
    parts = pieces(jnp.broadcast_to(line, (8, 512)), 3)
    count = dot_last(ones, parts[0]) + dot_last(ones, parts[1]) + dot_last(ones, parts[2])
    top_inv_ref[...] = jnp.broadcast_to(
        1.0 / (count[:, 0:1] + shrink_ref[0] * (TOTAL / TOP)), (TOP, 128)
    )
    cols_ref[...] = cols


def down_kernel(
    index_ref, shrink_ref, got_ref, middle_ref, parent3_ref, acc_ref, inv_ref, lines_ref, cols_ref, middle_turn_ref,
    top_turn_ref, third_inv_ref, top_inv_ref, down_ref, scale_ref, send_ref,
):
    left = iota((256, 128), 1) < PART
    weight_top = shrink_ref[0] * (TOTAL / TOP)
    weight_third = shrink_ref[1] * (TOTAL / THIRD)
    weight_middle = shrink_ref[2] * (TOTAL / 8192)
    weight_fine = shrink_ref[3]
    cols = cols_ref[...]
    top_id = iota((TOP, 256), 0)
    top_hot = jnp.concatenate(
        [hot(top_id == in_line(parent3_ref, 0, 2)), hot(top_id == in_line(parent3_ref, 2, 2))], axis=0
    )
    third_sums = got_ref[...].reshape(256, 128)
    top = two(dot(top_hot, side(third_sums, 2)))
    top = jnp.where(left[0:TOP], top[0:TOP], top[TOP : 2 * TOP])
    top = top + turned(top)
    center = jnp.sum(top, axis=0, keepdims=True) / TOTAL
    top_means = (top + weight_top * center) * top_inv_ref[...]
    term = two(dot(middle_turn_ref[...], side(third_sums * third_inv_ref[...], 2)))
    term = jnp.where(left, term[0:256], term[256:512])
    parts = side(top_means, 2)
    prior = term + turned(term) + scale_ref[...] * two(dot(down_ref[:, 0:TOP], parts))
    index = index_ref[0]
    rows = pl.ds(pl.multiple_of((index % 16) * 16, 16), 16)
    own = two(dot(top_turn_ref[pl.ds(pl.multiple_of(index * 16, 16), 16), 0:TOP], parts))
    own = (got_ref[pl.ds((index % 16) * 2, 2)].reshape(16, 128) + weight_third * own) * third_inv_ref[rows, :]
    own = jnp.where(index < 16, own, turned(own))
    inverse = jnp.concatenate([cols[:, 0:1], cols[:, 1:2]], axis=0)
    middle_means = (middle_ref[0:256, :] + weight_middle * prior) * inverse
    parts = side(middle_means, 2)
    left = left[0:128]
    lane = iota((128, 128), 1).astype(F32)
    lanes = (lane.astype(BF), (lane + 128.0).astype(BF))
    one, zero = jnp.array(1, BF), jnp.array(0, BF)
    halves = hot((iota((16, 256), 1) & 127) >> 6 == iota((16, 256), 0))
    for h in range(GROUPS):
        here = slice(128 * h, 128 * (h + 1))
        ones = []
        for b in range(2):
            parent = acc_ref[:, 2180 + 8 * h + b : 2181 + 8 * h + b]
            parent = jnp.broadcast_to(parent, (128, 128)).astype(BF)
            ones.append(
                jnp.concatenate([jnp.where(lane == parent, one, zero) for lane in lanes], axis=1)
            )
        found = two(dot(jnp.concatenate(ones, axis=0), parts))
        prior = jnp.where(left, found[0:128], found[128:256])
        sums = acc_ref[:, here]
        fine = ((sums + weight_fine * prior) * inv_ref[:, here]).astype(BF)
        send_ref[h, 0:128, :] = fine
        fine = fine.astype(F32)
        spread = (
            lines_ref[2 * h : 2 * h + 2]
            + lines_ref[32 + 2 * h : 34 + 2 * h] * dot_last(halves, side(fine * fine, 2))[0:2]
            - 2.0 * dot_last(halves, side(fine * sums, 2))[0:2]
        )
        send_ref[h, 128:144, :] = jnp.concatenate(
            [
                jnp.where(
                    left[0:8], middle_means[16 * h : 16 * h + 8], middle_means[16 * h + 8 : 16 * h + 16]
                ),
                own[h : h + 1],
            ]
            + [part.astype(F32) for part in pieces(spread, 3)]
            + [jnp.zeros((1, 128), F32)],
            axis=0,
        ).astype(BF)


def finish_kernel(got_ref, own_ref, out_ref, middle_ref, third_ref, spread_ref):
    left = iota((128, 128), 1) < PART
    total = jnp.zeros((8, 128), F32)
    for g in range(GROUPS // 2):
        here = slice(128 * g, 128 * (g + 1))
        a = got_ref[2 * g, 0:128, :].astype(F32)
        b = got_ref[2 * g + 1, 0:128, :].astype(F32)
        out_ref[0:128, here] = jnp.where(left, a, turned(b)).astype(BF)
        out_ref[128:256, here] = jnp.where(left, turned(a), b).astype(BF)
        a = got_ref[2 * g, 128:144, :].astype(F32)
        b = got_ref[2 * g + 1, 128:144, :].astype(F32)
        first = jnp.where(left[0:16], a, turned(b))
        second = jnp.where(left[0:16], turned(a), b)
        middle_ref[:, here] = jnp.concatenate([first[0:8], second[0:8]], axis=0).astype(BF)
        third_ref[:, here] = first[8:9].astype(BF)
        total = total + a[8:16] + b[8:16]
    total = total[1:3] + total[3:5] + total[5:7]
    spread_ref[...] = total / (WIDTH * (own_ref[0:2] + 1.0))


VMEM = pl.BlockSpec(memory_space=pltpu.VMEM)
SMEM = pl.BlockSpec(memory_space=pltpu.SMEM)
ANY = pl.BlockSpec(memory_space=pl.ANY)
DMA = pltpu.SemaphoreType.DMA


def call(kernel, limit, ins, outs, scratch=(), flops=0, moved=0):
    return pl.pallas_call(
        kernel,
        out_shape=[jax.ShapeDtypeStruct(s, d) for s, d in outs],
        in_specs=ins,
        out_specs=[VMEM] * len(outs),
        scratch_shapes=list(scratch),
        compiler_params=pltpu.CompilerParams(vmem_limit_bytes=limit * MIB),
        cost_estimate=pl.CostEstimate(flops=flops, bytes_accessed=moved, transcendentals=0),
    )


def exchange(x, axis):
    return lax.all_to_all(x, axis, split_axis=0, concat_axis=0, tiled=True)


def local(rows, fine_assign, parent1, parent2, parent3, shrink):
    index = jnp.stack([lax.axis_index("dp"), lax.axis_index("clus")]).astype(I32)
    parent2 = parent2.reshape(2, 128)
    parent3 = parent3.reshape(4, 128)
    block = ((GROUPS, ROWS, 128), BF)
    (send,) = call(pack_kernel, 60, [VMEM] * 3, [block])(
        rows, fine_assign.reshape(2, 128), parent1.reshape(2, 128)
    )
    group_rows = exchange(send, "clus")
    third, middle = call(
        middle_kernel,
        24,
        [VMEM, ANY],
        [((DP, 16, 128), BF), ((272, 128), F32)],
        [pltpu.VMEM((512, 2048), BF), pltpu.VMEM((2, 128), I32), DMA],
    )(group_rows, parent2)
    third = exchange(third, "dp")
    (sums,) = call(
        fine_kernel,
        24,
        [VMEM],
        [((128, 2304), F32)],
        [pltpu.VMEM((128, 128), F32), pltpu.VMEM((256, 2176), BF), pltpu.VMEM((128, 2176), F32)],
        4_000_000_000,
        4_000_000,
    )(group_rows)
    third, counts = call(share_kernel, 24, [VMEM, ANY], [((DP, 8, 128), F32), ((4, 128), F32)])(
        third, sums
    )
    third = exchange(third, "dp")
    *ready, own = call(
        ready_kernel,
        24,
        [SMEM, SMEM] + [VMEM] * 5,
        [
            ((128, 2048), F32),
            ((64, 128), F32),
            ((128, 128), F32),
            ((2 * MIDDLE, 256), BF),
            ((THIRD, 128), BF),
            ((256, 128), F32),
            ((TOP, 128), F32),
            ((256, 128), BF),
            ((256, 128), F32),
            ((8, 128), F32),
        ],
        (),
        1_000_000_000,
        8_000_000,
    )(index, shrink, sums, middle, counts, parent2, parent3)
    (send,) = call(down_kernel, 24, [SMEM, SMEM] + [VMEM] * 13, [block])(index, shrink, third, middle, parent3, sums, *ready)
    got = exchange(send, "clus")
    fine, middle, third, spread = call(
        finish_kernel,
        24,
        [VMEM, VMEM],
        [((256, 1024), BF), ((16, 1024), BF), ((1, 1024), BF), ((2, 128), F32)],
    )(got, own)
    return fine, middle, third, spread.reshape(256)


def solution(mesh):
    placed = (P(("dp", "clus"), None), P(("dp", "clus")), P(("dp", "clus")), P("dp"), P(), P())
    return jax.shard_map(
        local,
        mesh=mesh,
        in_specs=placed,
        out_specs=(
            P(("dp", "clus"), None),
            P(("dp", "clus"), None),
            P(("dp", "clus"), None),
            P(("dp", "clus")),
        ),
        check_vma=False,
    )
```

```python
import jax
import jax.numpy as jnp
from jax import lax
from jax.experimental import pallas as pl
from jax.experimental.pallas import tpu as pltpu
from jax.sharding import PartitionSpec as P

GROUPS = 16
DP = 32
FINE = 256
MIDDLE = 256
THIRD = 512
TOP = 64
WIDTH = 1024
PART = WIDTH // GROUPS
ROWS = 144
TOTAL = 131072.0
BF = jnp.bfloat16
F32 = jnp.float32
I32 = jnp.int32
MIB = 1024 * 1024


def iota(shape, dim):
    return lax.broadcasted_iota(I32, shape, dim)


def hot(mask):
    return jnp.where(mask, 1.0, 0.0).astype(BF)


def hot_row(down, row):
    return jnp.where(
        down == jnp.broadcast_to(row.astype(BF), down.shape), jnp.array(1, BF), jnp.array(0, BF)
    )


def pieces(x, count):
    out = []
    for k in range(count):
        part = x.astype(BF)
        out.append(part)
        if k + 1 < count:
            x = x - part.astype(F32)
    return out


def side(x, count):
    return jnp.concatenate(pieces(x, count), axis=1)


def turned(x):
    return pltpu.roll(x, PART, 1)


def dot(a, b):
    return jnp.dot(a, b, preferred_element_type=F32)


def dot_last(a, b):
    return lax.dot_general(a, b, (((1,), (1,)), ((), ())), preferred_element_type=F32)


def two(x):
    return x[:, 0:128] + x[:, 128:256]


def in_line(ref, first, count):
    return jnp.concatenate([ref[first + k : first + k + 1, :] for k in range(count)], axis=1)


def pack_kernel(rows_ref, assign_ref, parent1_ref, send_ref):
    fine = assign_ref[...] & (GROUPS * FINE - 1)
    parent = parent1_ref[...] & (MIDDLE - 1)
    tile = jnp.concatenate(
        [
            (fine >> 8).astype(F32),
            (fine & (FINE - 1)).astype(F32),
            parent.astype(F32),
            jnp.zeros((10, 128), F32),
        ],
        axis=0,
    ).astype(BF)
    left = iota((128, 128), 1) < PART
    for g in range(GROUPS // 2):
        top = rows_ref[0:128, 128 * g : 128 * (g + 1)].astype(F32)
        low = rows_ref[128:256, 128 * g : 128 * (g + 1)].astype(F32)
        send_ref[2 * g, 0:128, :] = jnp.where(left, top, turned(low)).astype(BF)
        send_ref[2 * g + 1, 0:128, :] = jnp.where(left, turned(top), low).astype(BF)
        send_ref[2 * g, 128:144, :] = tile
        send_ref[2 * g + 1, 128:144, :] = tile


def middle_kernel(rows_ref, parent2_hbm, third_ref, middle_ref, hot_ref, parent2_ref, sem):
    copy = pltpu.make_async_copy(parent2_hbm, parent2_ref, sem)
    copy.start()
    left = iota((256, 128), 1) < PART
    tails = [rows_ref[s, 128:144, :].astype(F32)[0:8] for s in range(GROUPS)]
    table = jnp.concatenate(
        [jnp.concatenate([tail[k : k + 1] for tail in tails], axis=0) for k in (4, 5)], axis=1
    ).astype(BF)
    down = iota((256, 256), 0).astype(F32).astype(BF)
    owner = iota((GROUPS, 256), 0).astype(F32)
    for s in range(GROUPS):
        tail = tails[s]
        high = jnp.concatenate([tail[0:1], tail[1:2]], axis=1)
        low = jnp.concatenate([tail[2:3], tail[3:4]], axis=1)
        found = dot(table, hot_row(down, low))
        parent = jnp.sum(jnp.where(owner == high, found, 0.0), axis=0, keepdims=True)
        ones = hot_row(down, parent)
        hot_ref[0:256, 128 * s : 128 * (s + 1)] = ones[:, 0:128]
        hot_ref[256:512, 128 * s : 128 * (s + 1)] = ones[:, 128:256]
    both = dot(hot_ref[...], rows_ref[:, 0:128, :].reshape(GROUPS * 128, 128))
    middle = jnp.where(left, both[0:256], both[256:512])
    middle = middle + turned(middle)
    tally = dot_last(jnp.ones((8, 2048), BF), hot_ref[0:256] + hot_ref[256:512])
    middle_ref[0:256, :] = middle
    middle_ref[256:264, :] = tally[:, 0:128]
    middle_ref[264:272, :] = tally[:, 128:256]
    copy.wait()
    line = in_line(parent2_ref, 0, 2)
    third = iota((256, 256), 0)
    first = hot(third == line)
    second = hot(third + 256 == line)
    parts = side(middle, 2)
    sums = jnp.where(left, two(dot(first, parts)), two(dot(second, parts))).reshape(DP, 8, 128)
    high, low = pieces(tally, 2)
    counts = [dot_last(high, ones) + dot_last(low, ones) for ones in (first, second)]
    counts = jnp.concatenate(
        [count[0:1, 128 * i : 128 * (i + 1)] for count in counts for i in range(2)], axis=0
    )
    tail = jnp.concatenate([part.astype(F32) for part in pieces(counts, 2)], axis=0)
    tail = jnp.broadcast_to(tail[None], (DP, 8, 128))
    third_ref[...] = jnp.concatenate([sums, tail], axis=1).astype(BF)


def fine_kernel(rows_ref, out_ref, ids_ref, wide_ref, acc_ref):
    lane = iota((128, 128), 1)
    left = lane < PART
    half = jnp.where(left, 0.0, 1.0)
    group = lane >> 5
    down = iota((128, 128), 0)
    for s in range(GROUPS):
        ids_ref[8 * s : 8 * s + 8, :] = rows_ref[s, 128:144, :].astype(F32)[0:8]
    columns = jnp.transpose(ids_ref[...])
    out_ref[:, 2176:2304] = columns
    for s in range(GROUPS):
        x = rows_ref[s, 0:128, :].astype(F32)
        y = turned(x)
        ones = []
        for j in range(2):
            block = slice(128 * j, 128 * (j + 1))
            twice = jnp.where(left, x, y) if j == 0 else jnp.where(left, y, x)
            low = columns[:, 8 * s + 2 + j : 8 * s + 3 + j]
            key = 2.0 * columns[:, 8 * s + j : 8 * s + j + 1] + jnp.where(low >= 128.0, 1.0, 0.0)
            key = jnp.broadcast_to(key, (128, 128))
            place = (key - half).astype(BF)
            narrow = twice.astype(BF)
            for h in range(GROUPS):
                wide_ref[block, 128 * h : 128 * (h + 1)] = jnp.where(
                    place == jnp.array(2 * h, BF), narrow, jnp.array(0, BF)
                )
            square = 0.5 * jnp.sum(twice * twice, axis=1, keepdims=True)
            hi, mid, lo = [p.astype(F32) for p in pieces(jnp.broadcast_to(square, (128, 128)), 3)]
            value = jnp.where(group == 0, hi, jnp.where(group == 1, mid, jnp.where(group == 2, lo, 1.0)))
            wide_ref[block, 2048:2176] = jnp.where(
                (lane & 31) == key.astype(I32), value, 0.0
            ).astype(BF)
            within = ids_ref[8 * s + 2 + j : 8 * s + 3 + j, :].astype(I32) & 127
            ones.append(hot(down == within))
        part = dot(jnp.concatenate(ones, axis=1), wide_ref[...])
        if s == 0:
            acc_ref[...] = part
        elif s < GROUPS - 1:
            acc_ref[...] += part
        else:
            out_ref[:, 0:2176] = acc_ref[...] + part


def share_kernel(got_ref, acc_hbm, out_ref, count_ref):
    total = got_ref[0].astype(F32)
    for k in range(1, DP):
        total = total + got_ref[k].astype(F32)
    out_ref[...] = jnp.broadcast_to(total[None, 0:8], (DP, 8, 128))
    count_ref[...] = total[8:12] + total[12:16]


def ready_kernel(
    index_ref, shrink_ref, acc_ref, middle_ref, third_ref, parent2_ref, parent3_ref, inv_ref, lines_ref, cols_ref,
    middle_turn_ref, top_turn_ref, third_inv_ref, top_inv_ref, down_ref, scale_ref, own_ref,
):
    weight_third = shrink_ref[1] * (TOTAL / THIRD)
    weight_middle = shrink_ref[2] * (TOTAL / 8192)
    left = iota((128, 128), 1) < PART
    tail = acc_ref[:, 2048:2176]
    square = tail[:, 0:32] + tail[:, 32:64] + tail[:, 64:96]
    count = tail[:, 96:128]
    lines = jnp.transpose(jnp.concatenate([square, count, jnp.zeros((128, 64), F32)], axis=1))
    lines_ref[...] = lines[0:64]
    row = iota((32, 128), 0)
    own = [
        jnp.sum(jnp.where(row == 2 * index_ref[1] + b, lines[32:64], 0.0), axis=0, keepdims=True)
        for b in range(2)
    ]
    own_ref[...] = jnp.concatenate(own + [jnp.zeros((6, 128), F32)], axis=0)
    inverse = 1.0 / (count + shrink_ref[3])
    for h in range(GROUPS):
        inv_ref[:, 128 * h : 128 * (h + 1)] = jnp.where(
            left, inverse[:, 2 * h : 2 * h + 1], inverse[:, 2 * h + 1 : 2 * h + 2]
        )
    third = third_ref[...]
    cols = jnp.transpose(
        jnp.concatenate(
            [
                1.0 / (middle_ref[256:257, :] + weight_middle),
                1.0 / (middle_ref[264:265, :] + weight_middle),
                parent3_ref[...].astype(F32),
                parent2_ref[...].astype(F32),
                1.0 / (third + weight_third),
                jnp.zeros((116, 128), F32),
            ],
            axis=0,
        )
    )
    third_inv_ref[...] = jnp.concatenate(
        [jnp.where(left, cols[:, 8 + k : 9 + k], cols[:, 10 + k : 11 + k]) for k in range(2)], axis=0
    )
    across = iota((128, 256), 1)
    for k in range(2):
        parent = cols[:, 6 + k : 7 + k].astype(I32)
        for b in range(2):
            middle_turn_ref[256 * b + 128 * k : 256 * b + 128 * (k + 1), :] = hot(
                across + 256 * b == parent
            )
    for k in range(4):
        top_turn_ref[128 * k : 128 * (k + 1), :] = hot(
            across[:, 0:128] == cols[:, 2 + k : 3 + k].astype(I32)
        )
    down = jnp.zeros((256, 128), F32)
    scale = jnp.zeros((256, 128), F32)
    for b in range(2):
        turn = middle_turn_ref[256 * b : 256 * (b + 1), :]
        down = down + dot(turn, top_turn_ref[256 * b : 256 * (b + 1), :])
        column = jnp.concatenate([cols[:, 8 + 2 * b + k : 9 + 2 * b + k] for k in range(2)], axis=0)
        for part in pieces(jnp.broadcast_to(weight_third * column, (256, 128)), 3):
            scale = scale + dot(turn, part)
    down_ref[...] = down.astype(BF)
    scale_ref[...] = scale
    ones = hot(iota((TOP, 512), 0) == in_line(parent3_ref, 0, 4))
    line = jnp.concatenate([third[k : k + 1] for k in range(4)], axis=1)
    parts = pieces(jnp.broadcast_to(line, (8, 512)), 3)
    count = dot_last(ones, parts[0]) + dot_last(ones, parts[1]) + dot_last(ones, parts[2])
    top_inv_ref[...] = jnp.broadcast_to(
        1.0 / (count[:, 0:1] + shrink_ref[0] * (TOTAL / TOP)), (TOP, 128)
    )
    cols_ref[...] = cols


def down_kernel(
    index_ref, shrink_ref, got_ref, middle_ref, parent3_ref, acc_ref, inv_ref, lines_ref, cols_ref, middle_turn_ref,
    top_turn_ref, third_inv_ref, top_inv_ref, down_ref, scale_ref, send_ref,
):
    left = iota((256, 128), 1) < PART
    weight_top = shrink_ref[0] * (TOTAL / TOP)
    weight_third = shrink_ref[1] * (TOTAL / THIRD)
    weight_middle = shrink_ref[2] * (TOTAL / 8192)
    weight_fine = shrink_ref[3]
    cols = cols_ref[...]
    top_id = iota((TOP, 256), 0)
    top_hot = jnp.concatenate(
        [hot(top_id == in_line(parent3_ref, 0, 2)), hot(top_id == in_line(parent3_ref, 2, 2))], axis=0
    )
    third_sums = got_ref[...].reshape(256, 128)
    top = two(dot(top_hot, side(third_sums, 2)))
    top = jnp.where(left[0:TOP], top[0:TOP], top[TOP : 2 * TOP])
    top = top + turned(top)
    center = jnp.sum(top, axis=0, keepdims=True) / TOTAL
    top_means = (top + weight_top * center) * top_inv_ref[...]
    term = two(dot(middle_turn_ref[...], side(third_sums * third_inv_ref[...], 2)))
    term = jnp.where(left, term[0:256], term[256:512])
    parts = side(top_means, 2)
    prior = term + turned(term) + scale_ref[...] * two(dot(down_ref[:, 0:TOP], parts))
    index = index_ref[0]
    rows = pl.ds(pl.multiple_of((index % 16) * 16, 16), 16)
    own = two(dot(top_turn_ref[pl.ds(pl.multiple_of(index * 16, 16), 16), 0:TOP], parts))
    own = (got_ref[pl.ds((index % 16) * 2, 2)].reshape(16, 128) + weight_third * own) * third_inv_ref[rows, :]
    own = jnp.where(index < 16, own, turned(own))
    inverse = jnp.concatenate([cols[:, 0:1], cols[:, 1:2]], axis=0)
    middle_means = (middle_ref[0:256, :] + weight_middle * prior) * inverse
    parts = side(middle_means, 2)
    left = left[0:128]
    lane = iota((128, 128), 1).astype(F32)
    lanes = (lane.astype(BF), (lane + 128.0).astype(BF))
    one, zero = jnp.array(1, BF), jnp.array(0, BF)
    halves = hot((iota((16, 256), 1) & 127) >> 6 == iota((16, 256), 0))
    fourths = hot(iota((16, 256), 1) >> 6 == iota((16, 256), 0))
    for h in range(GROUPS):
        here = slice(128 * h, 128 * (h + 1))
        ones = []
        for b in range(2):
            parent = acc_ref[:, 2180 + 8 * h + b : 2181 + 8 * h + b]
            parent = jnp.broadcast_to(parent, (128, 128)).astype(BF)
            ones.append(
                jnp.concatenate([jnp.where(lane == parent, one, zero) for lane in lanes], axis=1)
            )
        found = two(dot(jnp.concatenate(ones, axis=0), parts))
        prior = jnp.where(left, found[0:128], found[128:256])
        sums = acc_ref[:, here]
        fine = ((sums + weight_fine * prior) * inv_ref[:, here]).astype(BF)
        send_ref[h, 0:128, :] = fine
    for h in range(GROUPS):
        here = slice(128 * h, 128 * (h + 1))
        sums = acc_ref[:, here]
        fine = send_ref[h, 0:128, :].astype(F32)
        square = pieces(fine * fine, 3)
        cross = pieces(fine * sums, 3)
        last = dot_last(fourths, jnp.concatenate([square[2], cross[2]], axis=1))
        square = dot_last(halves, jnp.concatenate(square[0:2], axis=1))[0:2] + last[0:2]
        cross = dot_last(halves, jnp.concatenate(cross[0:2], axis=1))[0:2] + last[2:4]
        counts = lines_ref[32 + 2 * h : 34 + 2 * h]
        spread = lines_ref[2 * h : 2 * h + 2] + counts * square - 2.0 * cross
        send_ref[h, 128:144, :] = jnp.concatenate(
            [
                jnp.where(
                    left[0:8], middle_means[16 * h : 16 * h + 8], middle_means[16 * h + 8 : 16 * h + 16]
                ),
                own[h : h + 1],
            ]
            + [part.astype(F32) for part in pieces(spread, 3)]
            + [jnp.zeros((1, 128), F32)],
            axis=0,
        ).astype(BF)


def finish_kernel(got_ref, own_ref, out_ref, middle_ref, third_ref, spread_ref):
    left = iota((128, 128), 1) < PART
    total = jnp.zeros((8, 128), F32)
    for g in range(GROUPS // 2):
        here = slice(128 * g, 128 * (g + 1))
        a = got_ref[2 * g, 0:128, :].astype(F32)
        b = got_ref[2 * g + 1, 0:128, :].astype(F32)
        out_ref[0:128, here] = jnp.where(left, a, turned(b)).astype(BF)
        out_ref[128:256, here] = jnp.where(left, turned(a), b).astype(BF)
        a = got_ref[2 * g, 128:144, :].astype(F32)
        b = got_ref[2 * g + 1, 128:144, :].astype(F32)
        first = jnp.where(left[0:16], a, turned(b))
        second = jnp.where(left[0:16], turned(a), b)
        middle_ref[:, here] = jnp.concatenate([first[0:8], second[0:8]], axis=0).astype(BF)
        third_ref[:, here] = first[8:9].astype(BF)
        total = total + a[8:16] + b[8:16]
    total = total[1:3] + total[3:5] + total[5:7]
    spread_ref[...] = total / (WIDTH * (own_ref[0:2] + 1.0))


VMEM = pl.BlockSpec(memory_space=pltpu.VMEM)
SMEM = pl.BlockSpec(memory_space=pltpu.SMEM)
ANY = pl.BlockSpec(memory_space=pl.ANY)
DMA = pltpu.SemaphoreType.DMA


def call(kernel, limit, ins, outs, scratch=(), flops=0, moved=0):
    return pl.pallas_call(
        kernel,
        out_shape=[jax.ShapeDtypeStruct(s, d) for s, d in outs],
        in_specs=ins,
        out_specs=[VMEM] * len(outs),
        scratch_shapes=list(scratch),
        compiler_params=pltpu.CompilerParams(vmem_limit_bytes=limit * MIB),
        cost_estimate=pl.CostEstimate(flops=flops, bytes_accessed=moved, transcendentals=0),
    )


def exchange(x, axis):
    return lax.all_to_all(x, axis, split_axis=0, concat_axis=0, tiled=True)


def local(rows, fine_assign, parent1, parent2, parent3, shrink):
    index = jnp.stack([lax.axis_index("dp"), lax.axis_index("clus")]).astype(I32)
    parent2 = parent2.reshape(2, 128)
    parent3 = parent3.reshape(4, 128)
    block = ((GROUPS, ROWS, 128), BF)
    (send,) = call(pack_kernel, 60, [VMEM] * 3, [block])(
        rows, fine_assign.reshape(2, 128), parent1.reshape(2, 128)
    )
    group_rows = exchange(send, "clus")
    third, middle = call(
        middle_kernel,
        24,
        [VMEM, ANY],
        [((DP, 16, 128), BF), ((272, 128), F32)],
        [pltpu.VMEM((512, 2048), BF), pltpu.VMEM((2, 128), I32), DMA],
    )(group_rows, parent2)
    third = exchange(third, "dp")
    (sums,) = call(
        fine_kernel,
        24,
        [VMEM],
        [((128, 2304), F32)],
        [pltpu.VMEM((128, 128), F32), pltpu.VMEM((256, 2176), BF), pltpu.VMEM((128, 2176), F32)],
        4_000_000_000,
        4_000_000,
    )(group_rows)
    third, counts = call(share_kernel, 24, [VMEM, ANY], [((DP, 8, 128), F32), ((4, 128), F32)])(
        third, sums
    )
    third = exchange(third, "dp")
    *ready, own = call(
        ready_kernel,
        24,
        [SMEM, SMEM] + [VMEM] * 5,
        [
            ((128, 2048), F32),
            ((64, 128), F32),
            ((128, 128), F32),
            ((2 * MIDDLE, 256), BF),
            ((THIRD, 128), BF),
            ((256, 128), F32),
            ((TOP, 128), F32),
            ((256, 128), BF),
            ((256, 128), F32),
            ((8, 128), F32),
        ],
        (),
        1_000_000_000,
        8_000_000,
    )(index, shrink, sums, middle, counts, parent2, parent3)
    (send,) = call(down_kernel, 24, [SMEM, SMEM] + [VMEM] * 13, [block])(index, shrink, third, middle, parent3, sums, *ready)
    got = exchange(send, "clus")
    fine, middle, third, spread = call(
        finish_kernel,
        24,
        [VMEM, VMEM],
        [((256, 1024), BF), ((16, 1024), BF), ((1, 1024), BF), ((2, 128), F32)],
    )(got, own)
    return fine, middle, third, spread.reshape(256)


def solution(mesh):
    placed = (P(("dp", "clus"), None), P(("dp", "clus")), P(("dp", "clus")), P("dp"), P(), P())
    return jax.shard_map(
        local,
        mesh=mesh,
        in_specs=placed,
        out_specs=(
            P(("dp", "clus"), None),
            P(("dp", "clus"), None),
            P(("dp", "clus"), None),
            P(("dp", "clus")),
        ),
        check_vma=False,
    )
```

```python
import jax
import jax.numpy as jnp
from jax import lax
from jax.experimental import pallas as pl
from jax.experimental.pallas import tpu as pltpu
from jax.sharding import PartitionSpec as P

GROUPS = 16
DP = 32
FINE = 256
MIDDLE = 256
THIRD = 512
TOP = 64
WIDTH = 1024
PART = WIDTH // GROUPS
ROWS = 144
TOTAL = 131072.0
BF = jnp.bfloat16
F32 = jnp.float32
I32 = jnp.int32
MIB = 1024 * 1024


def iota(shape, dim):
    return lax.broadcasted_iota(I32, shape, dim)


def hot(mask):
    return jnp.where(mask, 1.0, 0.0).astype(BF)


def hot_row(down, row):
    return jnp.where(
        down == jnp.broadcast_to(row.astype(BF), down.shape), jnp.array(1, BF), jnp.array(0, BF)
    )


def pieces(x, count):
    out = []
    for k in range(count):
        part = x.astype(BF)
        out.append(part)
        if k + 1 < count:
            x = x - part.astype(F32)
    return out


def side(x, count):
    return jnp.concatenate(pieces(x, count), axis=1)


def turned(x):
    return pltpu.roll(x, PART, 1)


def dot(a, b):
    return jnp.dot(a, b, preferred_element_type=F32)


def dot_last(a, b):
    return lax.dot_general(a, b, (((1,), (1,)), ((), ())), preferred_element_type=F32)


def two(x):
    return x[:, 0:128] + x[:, 128:256]


def in_line(ref, first, count):
    return jnp.concatenate([ref[first + k : first + k + 1, :] for k in range(count)], axis=1)


def pack_kernel(dp_ref, clus_ref, rows_ref, assign_ref, parent1_ref, send_ref):
    fine = assign_ref[...] & (GROUPS * FINE - 1)
    parent = parent1_ref[...] & (MIDDLE - 1)
    tile = jnp.concatenate(
        [
            (fine >> 8).astype(F32),
            (fine & (FINE - 1)).astype(F32),
            parent.astype(F32),
            jnp.zeros((10, 128), F32),
        ],
        axis=0,
    ).astype(BF)
    left = iota((128, 128), 1) < PART
    for g in range(GROUPS // 2):
        top = rows_ref[0:128, 128 * g : 128 * (g + 1)].astype(F32)
        low = rows_ref[128:256, 128 * g : 128 * (g + 1)].astype(F32)
        send_ref[2 * g, 0:128, :] = jnp.where(left, top, turned(low)).astype(BF)
        send_ref[2 * g + 1, 0:128, :] = jnp.where(left, turned(top), low).astype(BF)
        send_ref[2 * g, 128:144, :] = tile
        send_ref[2 * g + 1, 128:144, :] = tile


def middle_kernel(rows_ref, parent2_hbm, third_ref, middle_ref, hot_ref, parent2_ref, sem):
    copy = pltpu.make_async_copy(parent2_hbm, parent2_ref, sem)
    copy.start()
    left = iota((256, 128), 1) < PART
    tails = [rows_ref[s, 128:144, :].astype(F32)[0:8] for s in range(GROUPS)]
    table = jnp.concatenate(
        [jnp.concatenate([tail[k : k + 1] for tail in tails], axis=0) for k in (4, 5)], axis=1
    ).astype(BF)
    down = iota((256, 256), 0).astype(F32).astype(BF)
    owner = iota((GROUPS, 256), 0).astype(F32)
    for s in range(GROUPS):
        tail = tails[s]
        high = jnp.concatenate([tail[0:1], tail[1:2]], axis=1)
        low = jnp.concatenate([tail[2:3], tail[3:4]], axis=1)
        found = dot(table, hot_row(down, low))
        parent = jnp.sum(jnp.where(owner == high, found, 0.0), axis=0, keepdims=True)
        ones = hot_row(down, parent)
        hot_ref[0:256, 128 * s : 128 * (s + 1)] = ones[:, 0:128]
        hot_ref[256:512, 128 * s : 128 * (s + 1)] = ones[:, 128:256]
    both = dot(hot_ref[...], rows_ref[:, 0:128, :].reshape(GROUPS * 128, 128))
    middle = jnp.where(left, both[0:256], both[256:512])
    middle = middle + turned(middle)
    tally = dot_last(jnp.ones((8, 2048), BF), hot_ref[0:256] + hot_ref[256:512])
    middle_ref[0:256, :] = middle
    middle_ref[256:264, :] = tally[:, 0:128]
    middle_ref[264:272, :] = tally[:, 128:256]
    copy.wait()
    line = in_line(parent2_ref, 0, 2)
    third = iota((256, 256), 0)
    first = hot(third == line)
    second = hot(third + 256 == line)
    parts = side(middle, 2)
    sums = jnp.where(left, two(dot(first, parts)), two(dot(second, parts))).reshape(DP, 8, 128)
    third_ref[:, 0] = sums[:, 0:4]
    third_ref[:, 1] = sums[:, 4:8]
    high, low = pieces(tally, 2)
    for k, ones in enumerate((first, second)):
        count = dot_last(high, ones) + dot_last(low, ones)
        for i in range(2):
            third_ref[:, 2, 2 * k + i, :] = jnp.broadcast_to(
                count[0:1, 128 * i : 128 * (i + 1)], (DP, 128)
            )


def fine_kernel(rows_ref, count_hbm, out_ref, ids_ref, wide_ref, acc_ref):
    lane = iota((128, 128), 1)
    left = lane < PART
    half = jnp.where(left, 0.0, 1.0)
    group = lane >> 5
    down = iota((128, 128), 0)
    for s in range(GROUPS):
        ids_ref[8 * s : 8 * s + 8, :] = rows_ref[s, 128:144, :].astype(F32)[0:8]
    columns = jnp.transpose(ids_ref[...])
    out_ref[:, 2176:2304] = columns
    for s in range(GROUPS):
        x = rows_ref[s, 0:128, :].astype(F32)
        y = turned(x)
        ones = []
        for j in range(2):
            block = slice(128 * j, 128 * (j + 1))
            twice = jnp.where(left, x, y) if j == 0 else jnp.where(left, y, x)
            low = columns[:, 8 * s + 2 + j : 8 * s + 3 + j]
            key = 2.0 * columns[:, 8 * s + j : 8 * s + j + 1] + jnp.where(low >= 128.0, 1.0, 0.0)
            key = jnp.broadcast_to(key, (128, 128))
            place = (key - half).astype(BF)
            narrow = twice.astype(BF)
            for h in range(GROUPS):
                wide_ref[block, 128 * h : 128 * (h + 1)] = jnp.where(
                    place == jnp.array(2 * h, BF), narrow, jnp.array(0, BF)
                )
            square = 0.5 * jnp.sum(twice * twice, axis=1, keepdims=True)
            hi, mid, lo = [p.astype(F32) for p in pieces(jnp.broadcast_to(square, (128, 128)), 3)]
            value = jnp.where(group == 0, hi, jnp.where(group == 1, mid, jnp.where(group == 2, lo, 1.0)))
            wide_ref[block, 2048:2176] = jnp.where(
                (lane & 31) == key.astype(I32), value, 0.0
            ).astype(BF)
            within = ids_ref[8 * s + 2 + j : 8 * s + 3 + j, :].astype(I32) & 127
            ones.append(hot(down == within))
        part = dot(jnp.concatenate(ones, axis=1), wide_ref[...])
        if s == 0:
            acc_ref[...] = part
        elif s < GROUPS - 1:
            acc_ref[...] += part
        else:
            out_ref[:, 0:2176] = acc_ref[...] + part


def share_kernel(got_ref, out_ref, count_ref):
    total = got_ref[0]
    for k in range(1, DP):
        total = total + got_ref[k]
    sums = jnp.concatenate([total[0], total[1]], axis=0)
    out_ref[...] = jnp.broadcast_to(sums[None], (DP, 8, 128))
    count_ref[...] = total[2]


def ready_kernel(
    clus_ref, shrink_ref, acc_ref, middle_ref, third_ref, parent2_ref, parent3_ref, inv_ref, lines_ref, cols_ref,
    middle_turn_ref, top_turn_ref, third_inv_ref, top_inv_ref, down_ref, scale_ref, own_ref,
):
    weight_third = shrink_ref[1] * (TOTAL / THIRD)
    weight_middle = shrink_ref[2] * (TOTAL / 8192)
    left = iota((128, 128), 1) < PART
    tail = acc_ref[:, 2048:2176]
    square = tail[:, 0:32] + tail[:, 32:64] + tail[:, 64:96]
    count = tail[:, 96:128]
    lines = jnp.transpose(jnp.concatenate([square, count, jnp.zeros((128, 64), F32)], axis=1))
    lines_ref[...] = lines[0:64]
    row = iota((32, 128), 0)
    own = [
        jnp.sum(jnp.where(row == 2 * clus_ref[0] + b, lines[32:64], 0.0), axis=0, keepdims=True)
        for b in range(2)
    ]
    own_ref[...] = jnp.concatenate(own + [jnp.zeros((6, 128), F32)], axis=0)
    inverse = 1.0 / (count + shrink_ref[3])
    for h in range(GROUPS):
        inv_ref[:, 128 * h : 128 * (h + 1)] = jnp.where(
            left, inverse[:, 2 * h : 2 * h + 1], inverse[:, 2 * h + 1 : 2 * h + 2]
        )
    third = third_ref[...]
    cols = jnp.transpose(
        jnp.concatenate(
            [
                1.0 / (middle_ref[256:257, :] + weight_middle),
                1.0 / (middle_ref[264:265, :] + weight_middle),
                parent3_ref[...].astype(F32),
                parent2_ref[...].astype(F32),
                1.0 / (third + weight_third),
                jnp.zeros((116, 128), F32),
            ],
            axis=0,
        )
    )
    third_inv_ref[...] = jnp.concatenate(
        [jnp.where(left, cols[:, 8 + k : 9 + k], cols[:, 10 + k : 11 + k]) for k in range(2)], axis=0
    )
    across = iota((128, 256), 1)
    for k in range(2):
        parent = cols[:, 6 + k : 7 + k].astype(I32)
        for b in range(2):
            middle_turn_ref[256 * b + 128 * k : 256 * b + 128 * (k + 1), :] = hot(
                across + 256 * b == parent
            )
    for k in range(4):
        top_turn_ref[128 * k : 128 * (k + 1), :] = hot(
            across[:, 0:128] == cols[:, 2 + k : 3 + k].astype(I32)
        )
    down = jnp.zeros((256, 128), F32)
    scale = jnp.zeros((256, 128), F32)
    for b in range(2):
        turn = middle_turn_ref[256 * b : 256 * (b + 1), :]
        down = down + dot(turn, top_turn_ref[256 * b : 256 * (b + 1), :])
        column = jnp.concatenate([cols[:, 8 + 2 * b + k : 9 + 2 * b + k] for k in range(2)], axis=0)
        for part in pieces(jnp.broadcast_to(weight_third * column, (256, 128)), 3):
            scale = scale + dot(turn, part)
    down_ref[...] = down.astype(BF)
    scale_ref[...] = scale
    ones = hot(iota((TOP, 512), 0) == in_line(parent3_ref, 0, 4))
    line = jnp.concatenate([third[k : k + 1] for k in range(4)], axis=1)
    parts = pieces(jnp.broadcast_to(line, (8, 512)), 3)
    count = dot_last(ones, parts[0]) + dot_last(ones, parts[1]) + dot_last(ones, parts[2])
    top_inv_ref[...] = jnp.broadcast_to(
        1.0 / (count[:, 0:1] + shrink_ref[0] * (TOTAL / TOP)), (TOP, 128)
    )
    cols_ref[...] = cols


def down_kernel(
    dp_ref, shrink_ref, got_ref, middle_ref, parent3_ref, acc_ref, inv_ref, lines_ref, cols_ref, middle_turn_ref,
    top_turn_ref, third_inv_ref, top_inv_ref, down_ref, scale_ref, send_ref,
):
    left = iota((256, 128), 1) < PART
    weight_top = shrink_ref[0] * (TOTAL / TOP)
    weight_third = shrink_ref[1] * (TOTAL / THIRD)
    weight_middle = shrink_ref[2] * (TOTAL / 8192)
    weight_fine = shrink_ref[3]
    cols = cols_ref[...]
    top_id = iota((TOP, 256), 0)
    top_hot = jnp.concatenate(
        [hot(top_id == in_line(parent3_ref, 0, 2)), hot(top_id == in_line(parent3_ref, 2, 2))], axis=0
    )
    third_sums = got_ref[...].reshape(256, 128)
    top = two(dot(top_hot, side(third_sums, 2)))
    top = jnp.where(left[0:TOP], top[0:TOP], top[TOP : 2 * TOP])
    top = top + turned(top)
    center = jnp.sum(top, axis=0, keepdims=True) / TOTAL
    top_means = (top + weight_top * center) * top_inv_ref[...]
    term = two(dot(middle_turn_ref[...], side(third_sums * third_inv_ref[...], 2)))
    term = jnp.where(left, term[0:256], term[256:512])
    parts = side(top_means, 2)
    prior = term + turned(term) + scale_ref[...] * two(dot(down_ref[:, 0:TOP], parts))
    index = dp_ref[0]
    rows = pl.ds(pl.multiple_of((index % 16) * 16, 16), 16)
    own = two(dot(top_turn_ref[pl.ds(pl.multiple_of(index * 16, 16), 16), 0:TOP], parts))
    own = (got_ref[pl.ds((index % 16) * 2, 2)].reshape(16, 128) + weight_third * own) * third_inv_ref[rows, :]
    own = jnp.where(index < 16, own, turned(own))
    inverse = jnp.concatenate([cols[:, 0:1], cols[:, 1:2]], axis=0)
    middle_means = (middle_ref[0:256, :] + weight_middle * prior) * inverse
    parts = side(middle_means, 2)
    left = left[0:128]
    lane = iota((128, 128), 1).astype(F32)
    lanes = (lane.astype(BF), (lane + 128.0).astype(BF))
    one, zero = jnp.array(1, BF), jnp.array(0, BF)
    halves = hot((iota((16, 256), 1) & 127) >> 6 == iota((16, 256), 0))
    fourths = hot(iota((16, 256), 1) >> 6 == iota((16, 256), 0))
    for h in range(GROUPS):
        here = slice(128 * h, 128 * (h + 1))
        ones = []
        for b in range(2):
            parent = acc_ref[:, 2180 + 8 * h + b : 2181 + 8 * h + b]
            parent = jnp.broadcast_to(parent, (128, 128)).astype(BF)
            ones.append(
                jnp.concatenate([jnp.where(lane == parent, one, zero) for lane in lanes], axis=1)
            )
        found = two(dot(jnp.concatenate(ones, axis=0), parts))
        prior = jnp.where(left, found[0:128], found[128:256])
        sums = acc_ref[:, here]
        fine = ((sums + weight_fine * prior) * inv_ref[:, here]).astype(BF)
        send_ref[h, 0:128, :] = fine
    for h in range(GROUPS):
        here = slice(128 * h, 128 * (h + 1))
        sums = acc_ref[:, here]
        fine = send_ref[h, 0:128, :].astype(F32)
        square = pieces(fine * fine, 3)
        cross = pieces(fine * sums, 3)
        last = dot_last(fourths, jnp.concatenate([square[2], cross[2]], axis=1))
        square = dot_last(halves, jnp.concatenate(square[0:2], axis=1))[0:2] + last[0:2]
        cross = dot_last(halves, jnp.concatenate(cross[0:2], axis=1))[0:2] + last[2:4]
        counts = lines_ref[32 + 2 * h : 34 + 2 * h]
        spread = lines_ref[2 * h : 2 * h + 2] + counts * square - 2.0 * cross
        send_ref[h, 128:144, :] = jnp.concatenate(
            [
                jnp.where(
                    left[0:8], middle_means[16 * h : 16 * h + 8], middle_means[16 * h + 8 : 16 * h + 16]
                ),
                own[h : h + 1],
            ]
            + [part.astype(F32) for part in pieces(spread, 3)]
            + [jnp.zeros((1, 128), F32)],
            axis=0,
        ).astype(BF)


def finish_kernel(got_ref, own_ref, out_ref, middle_ref, third_ref, spread_ref):
    left = iota((128, 128), 1) < PART
    total = jnp.zeros((8, 128), F32)
    for g in range(GROUPS // 2):
        here = slice(128 * g, 128 * (g + 1))
        a = got_ref[2 * g, 0:128, :].astype(F32)
        b = got_ref[2 * g + 1, 0:128, :].astype(F32)
        out_ref[0:128, here] = jnp.where(left, a, turned(b)).astype(BF)
        out_ref[128:256, here] = jnp.where(left, turned(a), b).astype(BF)
        a = got_ref[2 * g, 128:144, :].astype(F32)
        b = got_ref[2 * g + 1, 128:144, :].astype(F32)
        first = jnp.where(left[0:16], a, turned(b))
        second = jnp.where(left[0:16], turned(a), b)
        middle_ref[:, here] = jnp.concatenate([first[0:8], second[0:8]], axis=0).astype(BF)
        third_ref[:, here] = first[8:9].astype(BF)
        total = total + a[8:16] + b[8:16]
    total = total[1:3] + total[3:5] + total[5:7]
    spread_ref[...] = total / (WIDTH * (own_ref[0:2] + 1.0))


VMEM = pl.BlockSpec(memory_space=pltpu.VMEM)
SMEM = pl.BlockSpec(memory_space=pltpu.SMEM)
ANY = pl.BlockSpec(memory_space=pl.ANY)
DMA = pltpu.SemaphoreType.DMA


def call(kernel, limit, ins, outs, scratch=(), flops=0, moved=0):
    return pl.pallas_call(
        kernel,
        out_shape=[jax.ShapeDtypeStruct(s, d) for s, d in outs],
        in_specs=ins,
        out_specs=[VMEM] * len(outs),
        scratch_shapes=list(scratch),
        compiler_params=pltpu.CompilerParams(vmem_limit_bytes=limit * MIB),
        cost_estimate=pl.CostEstimate(flops=flops, bytes_accessed=moved, transcendentals=0),
    )


def exchange(x, axis):
    return lax.all_to_all(x, axis, split_axis=0, concat_axis=0, tiled=True)


def local(rows, fine_assign, parent1, parent2, parent3, shrink):
    dp = lax.axis_index("dp").astype(I32).reshape(1)
    clus = lax.axis_index("clus").astype(I32).reshape(1)
    parent2 = parent2.reshape(2, 128)
    parent3 = parent3.reshape(4, 128)
    block = ((GROUPS, ROWS, 128), BF)
    (send,) = call(pack_kernel, 60, [SMEM] * 2 + [VMEM] * 3, [block])(
        dp, clus, rows, fine_assign.reshape(2, 128), parent1.reshape(2, 128)
    )
    group_rows = exchange(send, "clus")
    third, middle = call(
        middle_kernel,
        24,
        [VMEM, ANY],
        [((DP, 3, 4, 128), F32), ((272, 128), F32)],
        [pltpu.VMEM((512, 2048), BF), pltpu.VMEM((2, 128), I32), DMA],
    )(group_rows, parent2)
    third = exchange(third, "dp")
    third, counts = call(share_kernel, 24, [VMEM], [((DP, 8, 128), F32), ((4, 128), F32)])(third)
    third = exchange(third, "dp")
    (sums,) = call(
        fine_kernel,
        24,
        [VMEM, ANY],
        [((128, 2304), F32)],
        [pltpu.VMEM((128, 128), F32), pltpu.VMEM((256, 2176), BF), pltpu.VMEM((128, 2176), F32)],
        4_000_000_000,
        4_000_000,
    )(group_rows, counts)
    *ready, own = call(
        ready_kernel,
        24,
        [SMEM, SMEM] + [VMEM] * 5,
        [
            ((128, 2048), F32),
            ((64, 128), F32),
            ((128, 128), F32),
            ((2 * MIDDLE, 256), BF),
            ((THIRD, 128), BF),
            ((256, 128), F32),
            ((TOP, 128), F32),
            ((256, 128), BF),
            ((256, 128), F32),
            ((8, 128), F32),
        ],
        (),
        1_000_000_000,
        8_000_000,
    )(clus, shrink, sums, middle, counts, parent2, parent3)
    (send,) = call(down_kernel, 24, [SMEM, SMEM] + [VMEM] * 13, [block])(dp, shrink, third, middle, parent3, sums, *ready)
    got = exchange(send, "clus")
    fine, middle, third, spread = call(
        finish_kernel,
        24,
        [VMEM, VMEM],
        [((256, 1024), BF), ((16, 1024), BF), ((1, 1024), BF), ((2, 128), F32)],
    )(got, own)
    return fine, middle, third, spread.reshape(256)


def solution(mesh):
    placed = (P(("dp", "clus"), None), P(("dp", "clus")), P(("dp", "clus")), P("dp"), P(), P())
    return jax.shard_map(
        local,
        mesh=mesh,
        in_specs=placed,
        out_specs=(
            P(("dp", "clus"), None),
            P(("dp", "clus"), None),
            P(("dp", "clus"), None),
            P(("dp", "clus")),
        ),
        check_vma=False,
    )
```

```python
import jax
import jax.numpy as jnp
from jax import lax
from jax.experimental import pallas as pl
from jax.experimental.pallas import tpu as pltpu
from jax.sharding import PartitionSpec as P

GROUPS = 16
DP = 32
FINE = 256
MIDDLE = 256
THIRD = 512
TOP = 64
WIDTH = 1024
PART = WIDTH // GROUPS
ROWS = 144
TOTAL = 131072.0
BF = jnp.bfloat16
F32 = jnp.float32
I32 = jnp.int32
MIB = 1024 * 1024


def iota(shape, dim):
    return lax.broadcasted_iota(I32, shape, dim)


def hot(mask):
    return jnp.where(mask, 1.0, 0.0).astype(BF)


def hot_row(down, row):
    return jnp.where(
        down == jnp.broadcast_to(row.astype(BF), down.shape), jnp.array(1, BF), jnp.array(0, BF)
    )


def pieces(x, count):
    out = []
    for k in range(count):
        part = x.astype(BF)
        out.append(part)
        if k + 1 < count:
            x = x - part.astype(F32)
    return out


def side(x, count):
    return jnp.concatenate(pieces(x, count), axis=1)


def turned(x):
    return pltpu.roll(x, PART, 1)


def dot(a, b):
    return jnp.dot(a, b, preferred_element_type=F32)


def dot_last(a, b):
    return lax.dot_general(a, b, (((1,), (1,)), ((), ())), preferred_element_type=F32)


def two(x):
    return x[:, 0:128] + x[:, 128:256]


def in_line(ref, first, count):
    return jnp.concatenate([ref[first + k : first + k + 1, :] for k in range(count)], axis=1)


def pack_kernel(dp_ref, clus_ref, rows_ref, assign_ref, parent1_ref, send_ref):
    fine = assign_ref[...] & (GROUPS * FINE - 1)
    parent = parent1_ref[...] & (MIDDLE - 1)
    tile = jnp.concatenate(
        [
            (fine >> 8).astype(F32),
            (fine & (FINE - 1)).astype(F32),
            parent.astype(F32),
            jnp.zeros((10, 128), F32),
        ],
        axis=0,
    ).astype(BF)
    left = iota((128, 128), 1) < PART
    for g in range(GROUPS // 2):
        top = rows_ref[0:128, 128 * g : 128 * (g + 1)].astype(F32)
        low = rows_ref[128:256, 128 * g : 128 * (g + 1)].astype(F32)
        send_ref[2 * g, 0:128, :] = jnp.where(left, top, turned(low)).astype(BF)
        send_ref[2 * g + 1, 0:128, :] = jnp.where(left, turned(top), low).astype(BF)
        send_ref[2 * g, 128:144, :] = tile
        send_ref[2 * g + 1, 128:144, :] = tile


def middle_kernel(rows_ref, parent2_hbm, down_hbm, third_ref, middle_ref, hot_ref, parent2_ref, sem):
    copy = pltpu.make_async_copy(parent2_hbm, parent2_ref, sem)
    copy.start()
    left = iota((256, 128), 1) < PART
    tails = [rows_ref[s, 128:144, :].astype(F32)[0:8] for s in range(GROUPS)]
    table = jnp.concatenate(
        [jnp.concatenate([tail[k : k + 1] for tail in tails], axis=0) for k in (4, 5)], axis=1
    ).astype(BF)
    down = iota((256, 256), 0).astype(F32).astype(BF)
    owner = iota((GROUPS, 256), 0).astype(F32)
    for s in range(GROUPS):
        tail = tails[s]
        high = jnp.concatenate([tail[0:1], tail[1:2]], axis=1)
        low = jnp.concatenate([tail[2:3], tail[3:4]], axis=1)
        found = dot(table, hot_row(down, low))
        parent = jnp.sum(jnp.where(owner == high, found, 0.0), axis=0, keepdims=True)
        ones = hot_row(down, parent)
        hot_ref[0:256, 128 * s : 128 * (s + 1)] = ones[:, 0:128]
        hot_ref[256:512, 128 * s : 128 * (s + 1)] = ones[:, 128:256]
    both = dot(hot_ref[...], rows_ref[:, 0:128, :].reshape(GROUPS * 128, 128))
    middle = jnp.where(left, both[0:256], both[256:512])
    middle = middle + turned(middle)
    tally = dot_last(jnp.ones((8, 2048), BF), hot_ref[0:256] + hot_ref[256:512])
    middle_ref[0:256, :] = middle
    middle_ref[256:264, :] = tally[:, 0:128]
    middle_ref[264:272, :] = tally[:, 128:256]
    copy.wait()
    line = in_line(parent2_ref, 0, 2)
    third = iota((256, 256), 0)
    first = hot(third == line)
    second = hot(third + 256 == line)
    parts = side(middle, 2)
    sums = jnp.where(left, two(dot(first, parts)), two(dot(second, parts))).reshape(DP, 8, 128)
    third_ref[:, 0] = sums[:, 0:4]
    third_ref[:, 1] = sums[:, 4:8]
    high, low = pieces(tally, 2)
    for k, ones in enumerate((first, second)):
        count = dot_last(high, ones) + dot_last(low, ones)
        for i in range(2):
            third_ref[:, 2, 2 * k + i, :] = jnp.broadcast_to(
                count[0:1, 128 * i : 128 * (i + 1)], (DP, 128)
            )


def fine_kernel(rows_ref, count_ref, out_ref, same_ref, ids_ref, wide_ref, acc_ref):
    lane = iota((128, 128), 1)
    left = lane < PART
    half = jnp.where(left, 0.0, 1.0)
    group = lane >> 5
    down = iota((128, 128), 0)
    for s in range(GROUPS):
        ids_ref[8 * s : 8 * s + 8, :] = rows_ref[s, 128:144, :].astype(F32)[0:8]
    same_ref[...] = count_ref[...]
    columns = jnp.transpose(ids_ref[...])
    out_ref[:, 2176:2304] = columns
    for s in range(GROUPS):
        x = rows_ref[s, 0:128, :].astype(F32)
        y = turned(x)
        ones = []
        for j in range(2):
            block = slice(128 * j, 128 * (j + 1))
            twice = jnp.where(left, x, y) if j == 0 else jnp.where(left, y, x)
            low = columns[:, 8 * s + 2 + j : 8 * s + 3 + j]
            key = 2.0 * columns[:, 8 * s + j : 8 * s + j + 1] + jnp.where(low >= 128.0, 1.0, 0.0)
            key = jnp.broadcast_to(key, (128, 128))
            place = (key - half).astype(BF)
            narrow = twice.astype(BF)
            for h in range(GROUPS):
                wide_ref[block, 128 * h : 128 * (h + 1)] = jnp.where(
                    place == jnp.array(2 * h, BF), narrow, jnp.array(0, BF)
                )
            square = 0.5 * jnp.sum(twice * twice, axis=1, keepdims=True)
            hi, mid, lo = [p.astype(F32) for p in pieces(jnp.broadcast_to(square, (128, 128)), 3)]
            value = jnp.where(group == 0, hi, jnp.where(group == 1, mid, jnp.where(group == 2, lo, 1.0)))
            wide_ref[block, 2048:2176] = jnp.where(
                (lane & 31) == key.astype(I32), value, 0.0
            ).astype(BF)
            within = ids_ref[8 * s + 2 + j : 8 * s + 3 + j, :].astype(I32) & 127
            ones.append(hot(down == within))
        part = dot(jnp.concatenate(ones, axis=1), wide_ref[...])
        if s == 0:
            acc_ref[...] = part
        elif s < GROUPS - 1:
            acc_ref[...] += part
        else:
            out_ref[:, 0:2176] = acc_ref[...] + part


def share_kernel(got_ref, out_ref, count_ref):
    total = got_ref[0]
    for k in range(1, DP):
        total = total + got_ref[k]
    sums = jnp.concatenate([total[0], total[1]], axis=0)
    out_ref[...] = jnp.broadcast_to(sums[None], (DP, 8, 128))
    count_ref[...] = total[2]


def parents_kernel(parent2_ref, parent3_ref, middle_turn_ref, top_turn_ref, down_ref):
    cols = jnp.transpose(
        jnp.concatenate(
            [
                jnp.zeros((2, 128), F32),
                parent3_ref[...].astype(F32),
                parent2_ref[...].astype(F32),
                jnp.zeros((120, 128), F32),
            ],
            axis=0,
        )
    )
    across = iota((128, 256), 1)
    for k in range(2):
        parent = cols[:, 6 + k : 7 + k].astype(I32)
        for b in range(2):
            middle_turn_ref[256 * b + 128 * k : 256 * b + 128 * (k + 1), :] = hot(
                across + 256 * b == parent
            )
    for k in range(4):
        top_turn_ref[128 * k : 128 * (k + 1), :] = hot(
            across[:, 0:128] == cols[:, 2 + k : 3 + k].astype(I32)
        )
    down = jnp.zeros((256, 128), F32)
    for b in range(2):
        half = slice(256 * b, 256 * (b + 1))
        down = down + dot(middle_turn_ref[half, :], top_turn_ref[half, :])
    down_ref[...] = down.astype(BF)


def ready_kernel(
    clus_ref, shrink_ref, acc_ref, middle_ref, third_ref, parent3_ref, middle_turn_ref, inv_ref, lines_ref, cols_ref,
    third_inv_ref, top_inv_ref, scale_ref, own_ref,
):
    weight_third = shrink_ref[1] * (TOTAL / THIRD)
    weight_middle = shrink_ref[2] * (TOTAL / 8192)
    left = iota((128, 128), 1) < PART
    tail = acc_ref[:, 2048:2176]
    square = tail[:, 0:32] + tail[:, 32:64] + tail[:, 64:96]
    count = tail[:, 96:128]
    lines = jnp.transpose(jnp.concatenate([square, count, jnp.zeros((128, 64), F32)], axis=1))
    lines_ref[...] = lines[0:64]
    row = iota((32, 128), 0)
    own = [
        jnp.sum(jnp.where(row == 2 * clus_ref[0] + b, lines[32:64], 0.0), axis=0, keepdims=True)
        for b in range(2)
    ]
    own_ref[...] = jnp.concatenate(own + [jnp.zeros((6, 128), F32)], axis=0)
    inverse = 1.0 / (count + shrink_ref[3])
    for h in range(GROUPS):
        inv_ref[:, 128 * h : 128 * (h + 1)] = jnp.where(
            left, inverse[:, 2 * h : 2 * h + 1], inverse[:, 2 * h + 1 : 2 * h + 2]
        )
    third = third_ref[...]
    cols = jnp.transpose(
        jnp.concatenate(
            [
                1.0 / (middle_ref[256:257, :] + weight_middle),
                1.0 / (middle_ref[264:265, :] + weight_middle),
                jnp.zeros((6, 128), F32),
                1.0 / (third + weight_third),
                jnp.zeros((116, 128), F32),
            ],
            axis=0,
        )
    )
    third_inv_ref[...] = jnp.concatenate(
        [jnp.where(left, cols[:, 8 + k : 9 + k], cols[:, 10 + k : 11 + k]) for k in range(2)], axis=0
    )
    scale = jnp.zeros((256, 128), F32)
    for b in range(2):
        turn = middle_turn_ref[256 * b : 256 * (b + 1), :]
        column = jnp.concatenate([cols[:, 8 + 2 * b + k : 9 + 2 * b + k] for k in range(2)], axis=0)
        for part in pieces(jnp.broadcast_to(weight_third * column, (256, 128)), 3):
            scale = scale + dot(turn, part)
    scale_ref[...] = scale
    ones = hot(iota((TOP, 512), 0) == in_line(parent3_ref, 0, 4))
    line = jnp.concatenate([third[k : k + 1] for k in range(4)], axis=1)
    parts = pieces(jnp.broadcast_to(line, (8, 512)), 3)
    count = dot_last(ones, parts[0]) + dot_last(ones, parts[1]) + dot_last(ones, parts[2])
    top_inv_ref[...] = jnp.broadcast_to(
        1.0 / (count[:, 0:1] + shrink_ref[0] * (TOTAL / TOP)), (TOP, 128)
    )
    cols_ref[...] = cols


def down_kernel(
    dp_ref, shrink_ref, got_ref, middle_ref, parent3_ref, acc_ref, inv_ref, lines_ref, cols_ref, middle_turn_ref,
    top_turn_ref, third_inv_ref, top_inv_ref, down_ref, scale_ref, send_ref,
):
    left = iota((256, 128), 1) < PART
    weight_top = shrink_ref[0] * (TOTAL / TOP)
    weight_third = shrink_ref[1] * (TOTAL / THIRD)
    weight_middle = shrink_ref[2] * (TOTAL / 8192)
    weight_fine = shrink_ref[3]
    cols = cols_ref[...]
    top_id = iota((TOP, 256), 0)
    top_hot = jnp.concatenate(
        [hot(top_id == in_line(parent3_ref, 0, 2)), hot(top_id == in_line(parent3_ref, 2, 2))], axis=0
    )
    third_sums = got_ref[...].reshape(256, 128)
    top = two(dot(top_hot, side(third_sums, 2)))
    top = jnp.where(left[0:TOP], top[0:TOP], top[TOP : 2 * TOP])
    top = top + turned(top)
    center = jnp.sum(top, axis=0, keepdims=True) / TOTAL
    top_means = (top + weight_top * center) * top_inv_ref[...]
    term = two(dot(middle_turn_ref[...], side(third_sums * third_inv_ref[...], 2)))
    term = jnp.where(left, term[0:256], term[256:512])
    parts = side(top_means, 2)
    prior = term + turned(term) + scale_ref[...] * two(dot(down_ref[:, 0:TOP], parts))
    index = dp_ref[0]
    rows = pl.ds(pl.multiple_of((index % 16) * 16, 16), 16)
    own = two(dot(top_turn_ref[pl.ds(pl.multiple_of(index * 16, 16), 16), 0:TOP], parts))
    own = (got_ref[pl.ds((index % 16) * 2, 2)].reshape(16, 128) + weight_third * own) * third_inv_ref[rows, :]
    own = jnp.where(index < 16, own, turned(own))
    inverse = jnp.concatenate([cols[:, 0:1], cols[:, 1:2]], axis=0)
    middle_means = (middle_ref[0:256, :] + weight_middle * prior) * inverse
    parts = side(middle_means, 2)
    left = left[0:128]
    lane = iota((128, 128), 1).astype(F32)
    lanes = (lane.astype(BF), (lane + 128.0).astype(BF))
    one, zero = jnp.array(1, BF), jnp.array(0, BF)
    halves = hot((iota((16, 256), 1) & 127) >> 6 == iota((16, 256), 0))
    fourths = hot(iota((16, 256), 1) >> 6 == iota((16, 256), 0))
    for h in range(GROUPS):
        here = slice(128 * h, 128 * (h + 1))
        ones = []
        for b in range(2):
            parent = acc_ref[:, 2180 + 8 * h + b : 2181 + 8 * h + b]
            parent = jnp.broadcast_to(parent, (128, 128)).astype(BF)
            ones.append(
                jnp.concatenate([jnp.where(lane == parent, one, zero) for lane in lanes], axis=1)
            )
        found = two(dot(jnp.concatenate(ones, axis=0), parts))
        prior = jnp.where(left, found[0:128], found[128:256])
        sums = acc_ref[:, here]
        fine = ((sums + weight_fine * prior) * inv_ref[:, here]).astype(BF)
        send_ref[h, 0:128, :] = fine
    for h in range(GROUPS):
        here = slice(128 * h, 128 * (h + 1))
        sums = acc_ref[:, here]
        fine = send_ref[h, 0:128, :].astype(F32)
        square = pieces(fine * fine, 3)
        cross = pieces(fine * sums, 3)
        last = dot_last(fourths, jnp.concatenate([square[2], cross[2]], axis=1))
        square = dot_last(halves, jnp.concatenate(square[0:2], axis=1))[0:2] + last[0:2]
        cross = dot_last(halves, jnp.concatenate(cross[0:2], axis=1))[0:2] + last[2:4]
        counts = lines_ref[32 + 2 * h : 34 + 2 * h]
        spread = lines_ref[2 * h : 2 * h + 2] + counts * square - 2.0 * cross
        send_ref[h, 128:144, :] = jnp.concatenate(
            [
                jnp.where(
                    left[0:8], middle_means[16 * h : 16 * h + 8], middle_means[16 * h + 8 : 16 * h + 16]
                ),
                own[h : h + 1],
            ]
            + [part.astype(F32) for part in pieces(spread, 3)]
            + [jnp.zeros((1, 128), F32)],
            axis=0,
        ).astype(BF)


def finish_kernel(got_ref, own_ref, out_ref, middle_ref, third_ref, spread_ref):
    left = iota((128, 128), 1) < PART
    total = jnp.zeros((8, 128), F32)
    for g in range(GROUPS // 2):
        here = slice(128 * g, 128 * (g + 1))
        a = got_ref[2 * g, 0:128, :].astype(F32)
        b = got_ref[2 * g + 1, 0:128, :].astype(F32)
        out_ref[0:128, here] = jnp.where(left, a, turned(b)).astype(BF)
        out_ref[128:256, here] = jnp.where(left, turned(a), b).astype(BF)
        a = got_ref[2 * g, 128:144, :].astype(F32)
        b = got_ref[2 * g + 1, 128:144, :].astype(F32)
        first = jnp.where(left[0:16], a, turned(b))
        second = jnp.where(left[0:16], turned(a), b)
        middle_ref[:, here] = jnp.concatenate([first[0:8], second[0:8]], axis=0).astype(BF)
        third_ref[:, here] = first[8:9].astype(BF)
        total = total + a[8:16] + b[8:16]
    total = total[1:3] + total[3:5] + total[5:7]
    spread_ref[...] = total / (WIDTH * (own_ref[0:2] + 1.0))


VMEM = pl.BlockSpec(memory_space=pltpu.VMEM)
SMEM = pl.BlockSpec(memory_space=pltpu.SMEM)
ANY = pl.BlockSpec(memory_space=pl.ANY)
DMA = pltpu.SemaphoreType.DMA


def call(kernel, limit, ins, outs, scratch=(), flops=0, moved=0):
    return pl.pallas_call(
        kernel,
        out_shape=[jax.ShapeDtypeStruct(s, d) for s, d in outs],
        in_specs=ins,
        out_specs=[VMEM] * len(outs),
        scratch_shapes=list(scratch),
        compiler_params=pltpu.CompilerParams(vmem_limit_bytes=limit * MIB),
        cost_estimate=pl.CostEstimate(flops=flops, bytes_accessed=moved, transcendentals=0),
    )


def exchange(x, axis):
    return lax.all_to_all(x, axis, split_axis=0, concat_axis=0, tiled=True)


def local(rows, fine_assign, parent1, parent2, parent3, shrink):
    dp = lax.axis_index("dp").astype(I32).reshape(1)
    clus = lax.axis_index("clus").astype(I32).reshape(1)
    parent2 = parent2.reshape(2, 128)
    parent3 = parent3.reshape(4, 128)
    block = ((GROUPS, ROWS, 128), BF)
    (send,) = call(pack_kernel, 60, [SMEM] * 2 + [VMEM] * 3, [block])(
        dp, clus, rows, fine_assign.reshape(2, 128), parent1.reshape(2, 128)
    )
    middle_turn, top_turn, down = call(
        parents_kernel,
        24,
        [VMEM, VMEM],
        [((2 * MIDDLE, 256), BF), ((THIRD, 128), BF), ((256, 128), BF)],
        (),
        1_000_000_000,
        4_000_000,
    )(parent2, parent3)
    group_rows = exchange(send, "clus")
    third, middle = call(
        middle_kernel,
        24,
        [VMEM, ANY, ANY],
        [((DP, 3, 4, 128), F32), ((272, 128), F32)],
        [pltpu.VMEM((512, 2048), BF), pltpu.VMEM((2, 128), I32), DMA],
    )(group_rows, parent2, down)
    third = exchange(third, "dp")
    third, counts = call(share_kernel, 24, [VMEM], [((DP, 8, 128), F32), ((4, 128), F32)])(third)
    third = exchange(third, "dp")
    sums, counts = call(
        fine_kernel,
        24,
        [VMEM, VMEM],
        [((128, 2304), F32), ((4, 128), F32)],
        [pltpu.VMEM((128, 128), F32), pltpu.VMEM((256, 2176), BF), pltpu.VMEM((128, 2176), F32)],
        4_000_000_000,
        4_000_000,
    )(group_rows, counts)
    inv, lines, cols, third_inv, top_inv, scale, own = call(
        ready_kernel,
        24,
        [SMEM, SMEM] + [VMEM] * 5,
        [
            ((128, 2048), F32),
            ((64, 128), F32),
            ((128, 128), F32),
            ((256, 128), F32),
            ((TOP, 128), F32),
            ((256, 128), F32),
            ((8, 128), F32),
        ],
        (),
        1_000_000_000,
        8_000_000,
    )(clus, shrink, sums, middle, counts, parent3, middle_turn)
    (send,) = call(down_kernel, 24, [SMEM, SMEM] + [VMEM] * 13, [block])(
        dp, shrink, third, middle, parent3, sums, inv, lines, cols, middle_turn, top_turn, third_inv, top_inv, down, scale
    )
    got = exchange(send, "clus")
    fine, middle, third, spread = call(
        finish_kernel,
        24,
        [VMEM, VMEM],
        [((256, 1024), BF), ((16, 1024), BF), ((1, 1024), BF), ((2, 128), F32)],
    )(got, own)
    return fine, middle, third, spread.reshape(256)


def solution(mesh):
    placed = (P(("dp", "clus"), None), P(("dp", "clus")), P(("dp", "clus")), P("dp"), P(), P())
    return jax.shard_map(
        local,
        mesh=mesh,
        in_specs=placed,
        out_specs=(
            P(("dp", "clus"), None),
            P(("dp", "clus"), None),
            P(("dp", "clus"), None),
            P(("dp", "clus")),
        ),
        check_vma=False,
    )
```
